32 devices in a mesh: req: 8 (over z, x), tp: 4 (over y, core).
Axes of the slice: x: 2, y: 2, z: 4, core: 2. Of those that a mesh axis runs over, the one named last changes fastest.
Arguments:
- queries: bfloat16 [4, 256, 8192], P(None, 'req', 'tp'), may hold values from -8 to 8
- new_kv: bfloat16 [4, 256, 2, 1024], P(None, 'req', None, 'tp'), may hold values from -8 to 8
- prefill_page_pool: bfloat16 [2048, 2, 16, 1024], P('req', None, None, 'tp'), may hold values from -6 to 6
- page_table: int32 [256, 8], P('req'), may hold values from 0 to 255, as said below
- prompt_len: int32 [256], P('req'), may hold values from 1 to 128
- dest_device: int32 [256], P('req'), may hold values from 0 to 7, as said below
- ssm_state: float32 [256, 16, 16384], P('req', None, 'tp'), may hold values from -4 to 4
- conv_state: bfloat16 [256, 3, 16384], P('req', None, 'tp'), may hold values from -6 to 6
- mamba_x: bfloat16 [4, 256, 16384], P(None, 'req', 'tp'), may hold values from -6 to 6
- mamba_z: bfloat16 [4, 256, 16384], P(None, 'req', 'tp'), may hold values from -6 to 6
- conv_weight: float32 [4, 16384], P(None, 'tp'), may hold values from -3 to 3
- conv_bias: float32 [16384], P('tp'), may hold values from -0.5 to 0.5
- x_proj: bfloat16 [16384, 544], P('tp'), may hold values from -0.046875 to 0.046875
- dt_gain: float32 [512], replicated, may hold values from 0.25 to 1.75
- dt_proj: bfloat16 [512, 16384], P(None, 'tp'), may hold values from -0.25 to 0.25
- dt_bias: float32 [16384], P('tp'), may hold values from -3 to 0
- a_log: float32 [16, 16384], P(None, 'tp'), may hold values from -1 to 2.8
- skip_d: float32 [16384], P('tp'), may hold values from 0.5 to 1.5
Outputs:
- attn_out: bfloat16 [4, 256, 8192], P(None, 'req', 'tp')
- mamba_out: bfloat16 [4, 256, 16384], P(None, 'req', 'tp')
The draws below stay inside these ranges and needn't reach their ends.
Inputs may be any that keep to these rules, and one draw needn't show every extreme that they name: `dest_device`: each prefill device hands exactly 4 of its requests to every decode device. `page_table`: the entries of one prefill device's rows are distinct pages of its own pool; only the first ceil(prompt_len / 16) of a row hold the request's tokens.
All inputs are finite; a program needn't handle non-finite values.
Results may differ from the reference program's by a relative error of at most 0.01.
Values may be sent and summed in bfloat16 or wider, within the bound.
A program may use at most 128 MiB of HBM per device.

```python
import math
import jax
import jax.numpy as jnp
from jax import lax

QUERY_HEADS = 64
KEY_VALUE_HEADS = 8
HEAD_SIZE = 128
CH = 16384
STATE = 16
DT_RANK = 512
CONV = 4
DECODE_STEPS = 4
PAGE_TOKENS = 16
LMAX = 128
REQ_DEV = 32
PAGE_LIST_MAX = 8
RPP = 4
REQUEST_TOTAL = 256
N_REQ = 8
N_TP = 4


def shared_routes(key):
    device_keys = jax.random.split(key, N_REQ)

    def one_device(device_key):
        return jax.random.permutation(device_key, REQ_DEV)
    shuffled = jax.vmap(one_device)(device_keys)
    return (shuffled // RPP).reshape(REQUEST_TOTAL).astype(jnp.int32)


def draw_dest_device(key, part):
    return shared_routes(key)


def draw_prompt_len(key, part):
    destinations = shared_routes(key)
    key = jax.random.fold_in(key, 11)
    first, second, third_part = jax.random.split(key, 3)
    heavy_phase = jax.random.randint(first, (), 0, 8)
    heavy = destinations % 8 == heavy_phase
    caps = jnp.where(heavy, LMAX, max(LMAX // 4, 1))
    raw_draws = jax.random.randint(second, (REQUEST_TOTAL,), 0, 1 << 20)
    lengths = 1 + raw_draws % caps
    priority = jax.random.permutation(third_part, REQUEST_TOTAL)
    chosen = jnp.argmax(jnp.where(heavy, priority, -1))
    lengths = lengths.at[chosen].set(LMAX)
    return lengths.astype(jnp.int32)


def draw_page_table(key, part):
    key = jax.random.fold_in(key, 23)
    device_keys = jax.random.split(key, N_REQ)

    def one_device(device_key):
        return jax.random.permutation(device_key, REQ_DEV * PAGE_LIST_MAX)
    return jax.vmap(one_device)(device_keys).reshape(REQUEST_TOTAL, PAGE_LIST_MAX).astype(jnp.int32)


def draw_queries(key, part):
    key = jax.random.fold_in(key, 31)
    simple_value = jnp.clip(jax.random.normal(key, (DECODE_STEPS, REQUEST_TOTAL, QUERY_HEADS, HEAD_SIZE), jnp.float32), -8.0, 8.0)
    return simple_value.reshape(DECODE_STEPS, REQUEST_TOTAL, QUERY_HEADS * HEAD_SIZE).astype(jnp.bfloat16)


def draw_new_kv(key, part):
    key = jax.random.fold_in(key, 37)
    simple_value = jnp.clip(jax.random.normal(key, (DECODE_STEPS, REQUEST_TOTAL, 2, KEY_VALUE_HEADS, HEAD_SIZE), jnp.float32), -8.0, 8.0)
    return simple_value.reshape(DECODE_STEPS, REQUEST_TOTAL, 2, KEY_VALUE_HEADS * HEAD_SIZE).astype(jnp.bfloat16)


def shard_levels(own_key, dims, pieces, smallest, largest):
    gain, own = 1.0, jax.random.fold_in(own_key, 6)
    for axis_at, blocks in pieces:
        draws = jnp.exp(jax.random.uniform(jax.random.fold_in(own, axis_at), (blocks,), jnp.float32, smallest / len(pieces), largest / len(pieces)))
        gain = gain * jnp.repeat(draws, dims[axis_at] // blocks).reshape([-1 if axis == axis_at else 1 for axis in range(len(dims))])
    return gain


def gaussian(stream_key, extent, width, most, pieces=(), kind=jnp.bfloat16):
    factor_of = shard_levels(stream_key, extent, pieces, -0.22, 0.18) if pieces else 1.0
    drawn = jax.random.normal(stream_key, extent, jnp.float32) * width * factor_of
    return jnp.minimum(jnp.maximum(drawn, -most), most).astype(kind)


def setup_inputs(seed: int = 0) -> dict:
    seeds = jax.random.split(jax.random.key(seed), 19)
    return {
        "queries": draw_queries(jax.random.fold_in(seeds[18], 71), 0),
        "new_kv": draw_new_kv(jax.random.fold_in(seeds[18], 71), 0),
        "prefill_page_pool": gaussian(seeds[2], (REQUEST_TOTAL * PAGE_LIST_MAX, 2, PAGE_TOKENS, KEY_VALUE_HEADS * HEAD_SIZE), 1.0, 6.0, ((0, 8), (3, 4))),
        "page_table": draw_page_table(jax.random.fold_in(seeds[18], 71), 0),
        "prompt_len": draw_prompt_len(jax.random.fold_in(seeds[18], 71), 0),
        "dest_device": draw_dest_device(jax.random.fold_in(seeds[18], 71), 0),
        "ssm_state": gaussian(seeds[6], (REQUEST_TOTAL, STATE, CH), 0.5, 4.0, ((0, 8), (2, 4)), jnp.float32),
        "conv_state": gaussian(seeds[7], (REQUEST_TOTAL, CONV - 1, CH), 1.0, 6.0, ((0, 8), (2, 4))),
        "mamba_x": gaussian(seeds[8], (DECODE_STEPS, REQUEST_TOTAL, CH), 1.0, 6.0, ((1, 8), (2, 4))),
        "mamba_z": gaussian(seeds[9], (DECODE_STEPS, REQUEST_TOTAL, CH), 1.0, 6.0, ((1, 8), (2, 4))),
        "conv_weight": gaussian(seeds[10], (CONV, CH), CONV ** -0.5, 3.0, ((1, 4),), jnp.float32),
        "conv_bias": jnp.clip(jax.random.uniform(seeds[11], (CH,), jnp.float32, -0.5, 0.5) * shard_levels(seeds[11], (CH,), ((0, 4),), -0.4, 0.0), -0.5, 0.5),
        "x_proj": gaussian(seeds[12], (CH, DT_RANK + 2 * STATE), CH ** -0.5, 0.046875, ((0, 4),)),
        "dt_gain": jnp.clip(1.0 + 0.15 * jax.random.normal(seeds[13], (DT_RANK,), jnp.float32), 0.25, 1.75),
        "dt_proj": gaussian(seeds[14], (DT_RANK, CH), DT_RANK ** -0.5, 0.25, ((1, 4),)),
        "dt_bias": jnp.clip(-3.0 + 3.0 * jax.random.uniform(seeds[15], (CH,), jnp.float32) ** shard_levels(seeds[15], (CH,), ((0, 4),), -0.2, 0.2), -3.0, 0.0),
        "a_log": jnp.clip(-1.0 + 3.8 * jax.random.uniform(seeds[16], (STATE, CH), jnp.float32) ** shard_levels(seeds[16], (STATE, CH), ((1, 4),), -0.2, 0.2), -1.0, 2.8),
        "skip_d": jnp.clip(0.5 + 1.0 * jax.random.uniform(seeds[17], (CH,), jnp.float32) ** shard_levels(seeds[17], (CH,), ((0, 4),), -0.2, 0.2), 0.5, 1.5),
    }


EPSILON = 1e-06
HIGHEST = lax.Precision.HIGHEST

def source_rows(dest_device):
    targets = dest_device.reshape(N_REQ, REQ_DEV)
    earlier = jnp.arange(REQ_DEV)[None, :] < jnp.arange(REQ_DEV)[:, None]
    matching = targets[:, :, None] == targets[:, None, :]
    ranking = lax.optimization_barrier(jnp.sum(jnp.where(matching & earlier[None], 1, 0), axis=2)).astype(jnp.int32)
    devices = jnp.arange(N_REQ, dtype=jnp.int32)[:, None]
    slot_index = (targets * REQ_DEV + devices * RPP + ranking).reshape(REQUEST_TOTAL).astype(jnp.int32)
    everything = jnp.arange(REQUEST_TOTAL, dtype=jnp.int32)
    return jnp.zeros((REQUEST_TOTAL,), jnp.int32).at[slot_index].set(everything)

def attention(queries, new_kv, prefill_page_pool, page_table, prompt_len, source_row):
    group_width = QUERY_HEADS // KEY_VALUE_HEADS
    cache_len = PAGE_LIST_MAX * PAGE_TOKENS
    page_ids = (source_row // REQ_DEV * (REQ_DEV * PAGE_LIST_MAX))[:, None] + page_table[source_row]
    lengths = prompt_len[source_row]
    key_valid = jnp.arange(cache_len)[None, :] < lengths[:, None]
    causal = jnp.arange(DECODE_STEPS)[None, :] <= jnp.arange(DECODE_STEPS)[:, None]
    score_scale = 1.0 / math.sqrt(HEAD_SIZE)
    all_queries = queries.reshape(DECODE_STEPS, REQUEST_TOTAL, QUERY_HEADS, HEAD_SIZE)

    def single_head(head_index):
        first_col = head_index * HEAD_SIZE
        head_cache = lax.dynamic_slice_in_dim(prefill_page_pool, first_col, HEAD_SIZE, 3)
        picked = head_cache[page_ids]
        cache_keys = picked[:, :, 0].reshape(REQUEST_TOTAL, cache_len, HEAD_SIZE).astype(jnp.float32)
        cache_values = picked[:, :, 1].reshape(REQUEST_TOTAL, cache_len, HEAD_SIZE).astype(jnp.float32)
        fresh_kv = lax.dynamic_slice_in_dim(new_kv, first_col, HEAD_SIZE, 3).astype(jnp.float32)
        head_query = lax.dynamic_slice_in_dim(all_queries, head_index * group_width, group_width, 2).astype(jnp.float32)
        cached_scores = jnp.einsum('trgd,rsd->trgs', head_query, cache_keys, precision=HIGHEST) * score_scale
        cached_scores = jnp.where(key_valid[None, :, None, :], cached_scores, -jnp.inf)
        recent_scores = jnp.einsum('trgd,urd->trgu', head_query, fresh_kv[:, :, 0], precision=HIGHEST) * score_scale
        recent_scores = jnp.where(causal[:, None, None, :], recent_scores, -jnp.inf)
        scores = jnp.concatenate([cached_scores, recent_scores], axis=3)
        row_max = lax.optimization_barrier(jnp.max(scores, axis=3, keepdims=True))
        weights = jnp.exp(scores - row_max)
        row_total = lax.optimization_barrier(jnp.sum(weights, axis=3, keepdims=True))
        weighted = jnp.einsum('trgs,rsd->trgd', weights[..., :cache_len], cache_values, precision=HIGHEST)
        weighted = weighted + jnp.einsum('trgu,urd->trgd', weights[..., cache_len:], fresh_kv[:, :, 1], precision=HIGHEST)
        return weighted / row_total
    each_head_value = lax.map(single_head, jnp.arange(KEY_VALUE_HEADS, dtype=jnp.int32))
    return jnp.transpose(each_head_value, (1, 2, 0, 3, 4)).reshape(DECODE_STEPS, REQUEST_TOTAL, QUERY_HEADS * HEAD_SIZE).astype(jnp.bfloat16)

def mamba_layer(ssm_state, conv_state, mamba_x, mamba_z, conv_weight, conv_bias, x_proj, dt_gain, dt_proj, dt_bias, a_log, skip_d, source_row):
    window = jnp.concatenate([jnp.transpose(conv_state[source_row], (1, 0, 2)).astype(jnp.float32), mamba_x.astype(jnp.float32)], axis=0)
    convolved = conv_bias + sum((conv_weight[offset] * window[offset:offset + DECODE_STEPS] for offset in range(CONV)))
    conv_out = jax.nn.silu(convolved).astype(jnp.bfloat16)
    proj = jnp.dot(conv_out.reshape(DECODE_STEPS * REQUEST_TOTAL, CH), x_proj, preferred_element_type=jnp.float32).reshape(DECODE_STEPS, REQUEST_TOTAL, DT_RANK + 2 * STATE)
    dt_low = proj[..., :DT_RANK]
    b_coef = proj[..., DT_RANK:DT_RANK + STATE]
    c_coef = proj[..., DT_RANK + STATE:]
    normed = (dt_low * lax.rsqrt(lax.optimization_barrier(jnp.mean(dt_low * dt_low, axis=-1, keepdims=True)) + EPSILON) * dt_gain).astype(jnp.bfloat16)
    flat_normed = normed.reshape(DECODE_STEPS * REQUEST_TOTAL, DT_RANK)
    block_width = CH // N_TP

    def one_block(block_index):
        first_col = block_index * block_width
        proj_block = lax.dynamic_slice_in_dim(dt_proj, first_col, block_width, 1)
        bias_block = lax.dynamic_slice_in_dim(dt_bias, first_col, block_width, 0)
        step_rate = jax.nn.softplus(jnp.dot(flat_normed, proj_block, preferred_element_type=jnp.float32).reshape(DECODE_STEPS, REQUEST_TOTAL, block_width) + bias_block)
        decay_log = -jnp.exp(lax.dynamic_slice_in_dim(a_log, first_col, block_width, 1))
        inputs = lax.dynamic_slice_in_dim(conv_out, first_col, block_width, 2).astype(jnp.float32)
        gate_values = jax.nn.silu(lax.dynamic_slice_in_dim(mamba_z, first_col, block_width, 2).astype(jnp.float32))
        skip_block = lax.dynamic_slice_in_dim(skip_d, first_col, block_width, 0)
        hidden_state = lax.dynamic_slice_in_dim(ssm_state, first_col, block_width, 2)[source_row]
        outputs = []
        for moment in range(DECODE_STEPS):
            hidden_state = jnp.exp(step_rate[moment][:, None, :] * decay_log[None]) * hidden_state + (step_rate[moment] * inputs[moment])[:, None, :] * b_coef[moment][:, :, None]
            reading = lax.optimization_barrier(jnp.sum(c_coef[moment][:, :, None] * hidden_state, axis=1)) + skip_block * inputs[moment]
            outputs.append(reading * gate_values[moment])
        return jnp.stack(outputs)
    per_block = lax.map(one_block, jnp.arange(N_TP, dtype=jnp.int32))
    return jnp.transpose(per_block, (1, 2, 0, 3)).reshape(DECODE_STEPS, REQUEST_TOTAL, CH).astype(jnp.bfloat16)

def reference(queries, new_kv, prefill_page_pool, page_table, prompt_len, dest_device, ssm_state, conv_state, mamba_x, mamba_z, conv_weight, conv_bias, x_proj, dt_gain, dt_proj, dt_bias, a_log, skip_d):
    source_row = source_rows(dest_device)
    attn_out = attention(queries, new_kv, prefill_page_pool, page_table, prompt_len, source_row)
    mamba_out = mamba_layer(ssm_state, conv_state, mamba_x, mamba_z, conv_weight, conv_bias, x_proj, dt_gain, dt_proj, dt_bias, a_log, skip_d, source_row)
    return (attn_out, mamba_out)
```

```python
import math

import jax
import jax.numpy as jnp
from jax import lax
from jax.sharding import PartitionSpec as P

HEAD_SIZE = 128


EPSILON = 1e-06
HIGHEST = lax.Precision.HIGHEST


def cached_part(grouped, cache_keys, cache_values, key_valid, score_scale):
    scores = (
        jnp.einsum("trkgd,rskd->trkgs", grouped, cache_keys, preferred_element_type=jnp.float32)
        * score_scale
    )
    scores = jnp.where(key_valid[None, :, None, None, :], scores, -jnp.inf)
    row_max = jnp.max(scores, axis=4)
    weights = jnp.exp(scores - row_max[..., None])
    row_total = jnp.sum(weights, axis=4)
    weighted = jnp.einsum(
        "trkgs,rskd->trkgd", weights, cache_values.astype(jnp.float32), precision=HIGHEST
    )
    return (weighted, row_max, row_total)


def recent_part(grouped, fresh_kv, score_scale):
    step_count = grouped.shape[0]
    scores = (
        jnp.einsum(
            "trkgd,urkd->trkgu", grouped, fresh_kv[:, :, 0], preferred_element_type=jnp.float32
        )
        * score_scale
    )
    causal = jnp.arange(step_count)[None, :] <= jnp.arange(step_count)[:, None]
    scores = jnp.where(causal[:, None, None, None, :], scores, -jnp.inf)
    row_max = jnp.max(scores, axis=4)
    weights = jnp.exp(scores - row_max[..., None])
    row_total = jnp.sum(weights, axis=4)
    weighted = jnp.einsum(
        "trkgu,urkd->trkgd", weights, fresh_kv[:, :, 1].astype(jnp.float32), precision=HIGHEST
    )
    return (weighted, row_max, row_total)


def sum_over_tp(value):
    width = lax.axis_size("tp")
    hop = 1
    while hop < width:
        pairs = [(index, index ^ hop) for index in range(width)]
        value = value + lax.ppermute(value, "tp", pairs)
        hop *= 2
    return value


def swap_rows(value):
    return lax.all_to_all(value, "req", split_axis=1, concat_axis=1, tiled=True)


def mamba_readings(
    start_state, conv_rows, rows_x, conv_weight, conv_bias, x_proj, dt_gain, dt_proj, dt_bias, a_log, skip_d
):
    step_count = rows_x.shape[0]
    tap_count = conv_weight.shape[0]
    rank_width = dt_proj.shape[0]
    state_size = a_log.shape[0]
    window = jnp.concatenate([jnp.transpose(conv_rows, (1, 0, 2)), rows_x], axis=0).astype(jnp.float32)
    convolved = conv_bias + sum(
        (conv_weight[offset] * window[offset : offset + step_count] for offset in range(tap_count))
    )
    conv_out = jax.nn.silu(convolved).astype(jnp.bfloat16)
    inputs = conv_out.astype(jnp.float32)
    decay_log = -jnp.exp(a_log)
    proj = sum_over_tp(
        jnp.einsum("trc,cw->trw", conv_out, x_proj, preferred_element_type=jnp.float32)
    )
    dt_low = proj[..., :rank_width]
    b_coef = proj[..., rank_width : rank_width + state_size]
    c_coef = proj[..., rank_width + state_size :]
    normed = (
        dt_low
        * lax.rsqrt(jnp.mean(dt_low * dt_low, axis=-1, keepdims=True) + EPSILON)
        * dt_gain
    ).astype(jnp.bfloat16)
    step_rate = jax.nn.softplus(
        jnp.einsum("trk,kc->trc", normed, dt_proj, preferred_element_type=jnp.float32) + dt_bias
    )
    hidden_state = start_state
    outputs = []
    for moment in range(step_count):
        rate = step_rate[moment]
        hidden_state = (
            jnp.exp(rate[:, None, :] * decay_log[None]) * hidden_state
            + (rate * inputs[moment])[:, None, :] * b_coef[moment][:, :, None]
        )
        reading = jnp.sum(c_coef[moment][:, :, None] * hidden_state, axis=1) + skip_d * inputs[moment]
        outputs.append(reading)
    return jnp.stack(outputs)


def per_device(
    queries,
    new_kv,
    prefill_page_pool,
    page_table,
    prompt_len,
    dest_device,
    ssm_state,
    conv_state,
    mamba_x,
    mamba_z,
    conv_weight,
    conv_bias,
    x_proj,
    dt_gain,
    dt_proj,
    dt_bias,
    a_log,
    skip_d,
):
    local_reqs = dest_device.shape[0]
    step_count = queries.shape[0]
    kv_heads = prefill_page_pool.shape[3] // HEAD_SIZE
    q_heads = queries.shape[2] // HEAD_SIZE
    group_width = q_heads // kv_heads
    cache_len = page_table.shape[1] * prefill_page_pool.shape[2]
    score_scale = 1.0 / math.sqrt(HEAD_SIZE)
    share = local_reqs // lax.axis_size("req")
    index = jnp.arange(local_reqs, dtype=jnp.int32)
    same = dest_device[:, None] == dest_device[None, :]
    rank = jnp.sum((same & (index[None, :] < index[:, None])).astype(jnp.int32), axis=1)
    slot = dest_device * share + rank
    to_home = (slot[:, None] == index[None, :]).astype(jnp.bfloat16)
    moved_x = swap_rows(mamba_x)
    moved_q = swap_rows(queries)
    moved_kv = swap_rows(new_kv.reshape(step_count, local_reqs, -1))
    rows_x = jnp.einsum("ks,tsc->tkc", to_home, moved_x)
    rows_q = jnp.einsum("ks,tsc->tkc", to_home, moved_q)
    rows_kv = jnp.einsum("ks,tsc->tkc", to_home, moved_kv)
    readings = mamba_readings(
        ssm_state, conv_state, rows_x, conv_weight, conv_bias, x_proj, dt_gain, dt_proj, dt_bias, a_log, skip_d
    ).astype(jnp.bfloat16)
    back_y = swap_rows(jnp.einsum("ks,tkc->tsc", to_home, readings))
    grouped = rows_q.reshape(step_count, local_reqs, kv_heads, group_width, HEAD_SIZE)
    fresh_kv = rows_kv.reshape(step_count, local_reqs, 2, kv_heads, HEAD_SIZE)
    picked = prefill_page_pool[page_table]
    key_valid = jnp.arange(cache_len)[None, :] < prompt_len[:, None]
    cache_keys = picked[:, :, 0].reshape(local_reqs, cache_len, kv_heads, HEAD_SIZE)
    cache_values = picked[:, :, 1].reshape(local_reqs, cache_len, kv_heads, HEAD_SIZE)
    weighted, row_max, row_total = cached_part(
        grouped, cache_keys, cache_values, key_valid, score_scale
    )
    recent_weighted, recent_max, recent_total = recent_part(grouped, fresh_kv, score_scale)
    joint_max = jnp.maximum(row_max, recent_max)
    old_weight = jnp.exp(row_max - joint_max)
    new_weight = jnp.exp(recent_max - joint_max)
    combined = weighted * old_weight[..., None] + recent_weighted * new_weight[..., None]
    combined = combined / (row_total * old_weight + recent_total * new_weight)[..., None]
    rows_out = combined.reshape(step_count, local_reqs, q_heads * HEAD_SIZE).astype(jnp.bfloat16)
    attn_out = swap_rows(jnp.einsum("ks,tkc->tsc", to_home, rows_out))
    gate_values = jax.nn.silu(mamba_z.astype(jnp.float32))
    mamba_out = (back_y.astype(jnp.float32) * gate_values).astype(jnp.bfloat16)
    return (attn_out, mamba_out)


def solution(mesh):
    return jax.shard_map(
        per_device,
        mesh=mesh,
        in_specs=(
            P(None, "req", "tp"),
            P(None, "req", None, "tp"),
            P("req", None, None, "tp"),
            P("req", None),
            P("req"),
            P("req"),
            P("req", None, "tp"),
            P("req", None, "tp"),
            P(None, "req", "tp"),
            P(None, "req", "tp"),
            P(None, "tp"),
            P("tp"),
            P("tp", None),
            P(),
            P(None, "tp"),
            P("tp"),
            P(None, "tp"),
            P("tp"),
        ),
        out_specs=(P(None, "req", "tp"), P(None, "req", "tp")),
        check_vma=False,
    )
```

```python
import functools
import math

import jax
import jax.numpy as jnp
from jax import lax
from jax.experimental import pallas as pl
from jax.experimental.pallas import tpu as pltpu
from jax.sharding import PartitionSpec as P

HEAD_SIZE = 128
BLOCK_ROWS = 16
EPSILON = 1e-06
LOG2E = 1.4426950408889634
VMEM_LIMIT = 48 * 1024 * 1024
MESH = pl.DeviceIdType.MESH
ANY = pl.BlockSpec(memory_space=pl.ANY)
VMEM = pl.BlockSpec(memory_space=pltpu.VMEM)


def greet(axes):
    barrier = pltpu.get_barrier_semaphore()
    total = 0
    for name in axes:
        size = lax.axis_size(name)
        me = lax.axis_index(name)
        for step in range(1, size):
            pl.semaphore_signal(
                barrier, inc=1, device_id={name: lax.rem(me + step, size)}, device_id_type=MESH
            )
        total += size - 1
    pl.semaphore_wait(barrier, total)


def remote(src, dst, send_sem, recv_sem, axis, peer):
    return pltpu.make_async_remote_copy(
        src_ref=src,
        dst_ref=dst,
        send_sem=send_sem,
        recv_sem=recv_sem,
        device_id={axis: peer},
        device_id_type=MESH,
    )


def front_kernel(
    xb,
    qb,
    conv_rows,
    place,
    conv_weight,
    conv_bias,
    x_proj,
    dt_gain,
    conv_out,
    normed,
    coefs,
    q_out,
    x_in,
    proj_w,
    part,
    gathered,
    x_send,
    x_recv,
    q_send,
    q_recv,
    local_sem,
    rs_send,
    rs_recv,
    ag_send,
    ag_recv,
):
    n = lax.axis_size("req")
    width = lax.axis_size("tp")
    me = lax.axis_index("req")
    lane = lax.axis_index("tp")
    splits, rows, _ = place.shape
    block_width = xb.shape[2]
    local_reqs = conv_rows.shape[1]
    steps = rows // local_reqs
    taps = conv_weight.shape[0]
    rank_width = dt_gain.shape[1]
    proj_width = x_proj.shape[1]
    piece = rows // width
    weights_copy = pltpu.make_async_copy(x_proj, proj_w, local_sem.at[0])
    weights_copy.start()
    own_x = pltpu.make_async_copy(xb.at[me], x_in.at[me], local_sem.at[1])
    own_x.start()
    own_q = pltpu.make_async_copy(qb.at[me], q_out.at[me], local_sem.at[2])
    own_q.start()
    greet(("req", "tp"))
    x_copies, q_copies = [], []
    for step in range(1, n):
        peer = lax.rem(me + step, n)
        x_copies.append(
            remote(xb.at[peer], x_in.at[me], x_send.at[step], x_recv.at[step], "req", peer)
        )
        x_copies[-1].start()
    for step in range(1, n):
        peer = lax.rem(me + step, n)
        q_copies.append(
            remote(qb.at[peer], q_out.at[me], q_send.at[step], q_recv.at[step], "req", peer)
        )
        q_copies[-1].start()
    part[...] = jnp.zeros_like(part)
    own_x.wait()
    weights_copy.wait()
    for copy in x_copies:
        copy.wait()
    chunk = min(512, block_width)
    for split in range(splits):

        def one_chunk(at, carry):
            inner = pl.ds(pl.multiple_of(at * chunk, chunk), chunk)
            outer = pl.ds(pl.multiple_of(split * block_width + at * chunk, chunk), chunk)
            block = x_in[:, :, inner].reshape(n * BLOCK_ROWS, chunk)
            fresh = jnp.dot(place[split], block, preferred_element_type=jnp.float32)
            window = [conv_rows[row, :, outer].astype(jnp.float32) for row in range(taps - 1)]
            window += [fresh[t * local_reqs : (t + 1) * local_reqs] for t in range(steps)]
            for t in range(steps):
                total = conv_bias[:, outer] + sum(
                    conv_weight[tap : tap + 1, outer] * window[t + tap] for tap in range(taps)
                )
                active = total / (1.0 + jnp.exp(-total))
                conv_out[t * local_reqs : (t + 1) * local_reqs, outer] = active.astype(jnp.bfloat16)
            part[:, :proj_width] += jnp.dot(
                conv_out[:, outer], proj_w[outer, :], preferred_element_type=jnp.float32
            )
            return carry

        lax.fori_loop(0, block_width // chunk, one_chunk, 0)
    copies = []
    for step in range(1, width):
        peer = lax.rem(lane + step, width)
        copies.append(
            remote(
                part.at[pl.ds(pl.multiple_of(peer * piece, piece), piece)],
                gathered.at[step],
                rs_send.at[step],
                rs_recv.at[step],
                "tp",
                peer,
            )
        )
        copies[-1].start()
    mine = pl.ds(pl.multiple_of(lane * piece, piece), piece)
    gathered[0] = part[mine, :]
    for copy in copies:
        copy.wait()
    summed = gathered[0]
    for step in range(1, width):
        summed = summed + gathered[step]
    dt_low = summed[:, :rank_width]
    scale = lax.rsqrt(jnp.mean(dt_low * dt_low, axis=-1, keepdims=True) + EPSILON)
    normed[mine, :] = (dt_low * scale * dt_gain[...]).astype(jnp.bfloat16)
    coefs[mine, :] = summed[:, rank_width:]
    copies = []
    for step in range(1, width):
        peer = lax.rem(lane + step, width)
        for at, ref in enumerate((normed, coefs)):
            copies.append(
                remote(
                    ref.at[mine], ref.at[mine], ag_send.at[at, step], ag_recv.at[at, step], "tp", peer
                )
            )
            copies[-1].start()
    for copy in copies:
        copy.wait()
    own_q.wait()
    for copy in q_copies:
        copy.wait()


def front(xb, qb, conv_rows, place, conv_weight, conv_bias, x_proj, dt_gain):
    n = xb.shape[0]
    width = lax.axis_size("tp")
    rows = place.shape[1]
    channels = conv_weight.shape[1]
    rank_width = dt_gain.shape[1]
    wide = rank_width + 128
    dma = pltpu.SemaphoreType.DMA
    return pl.pallas_call(
        front_kernel,
        out_shape=(
            jax.ShapeDtypeStruct((rows, channels), jnp.bfloat16),
            jax.ShapeDtypeStruct((rows, rank_width), jnp.bfloat16),
            jax.ShapeDtypeStruct((rows, 128), jnp.float32),
            jax.ShapeDtypeStruct(qb.shape, qb.dtype),
        ),
        in_specs=[ANY, ANY, VMEM, VMEM, VMEM, VMEM, ANY, VMEM],
        out_specs=(VMEM, VMEM, VMEM, ANY),
        scratch_shapes=[
            pltpu.VMEM(xb.shape, xb.dtype),
            pltpu.VMEM(x_proj.shape, x_proj.dtype),
            pltpu.VMEM((rows, wide), jnp.float32),
            pltpu.VMEM((width, rows // width, wide), jnp.float32),
            dma((n,)),
            dma((n,)),
            dma((n,)),
            dma((n,)),
            dma((3,)),
            dma((width,)),
            dma((width,)),
            dma((2, width)),
            dma((2, width)),
        ],
        compiler_params=pltpu.CompilerParams(
            collective_id=0, has_side_effects=True, vmem_limit_bytes=VMEM_LIMIT
        ),
    )(xb, qb, conv_rows, place, conv_weight, conv_bias, x_proj, dt_gain)


def attention_kernel(
    kv_heads, q_rows, steps, table, lengths, slots, slabs, pool, out, pages, page_sem
):
    local_reqs, list_len = table.shape
    page_tokens = pool.shape[2]
    cache_len = list_len * page_tokens
    scale = 1.0 / math.sqrt(HEAD_SIZE)
    recent = kv_heads * steps
    group_width = q_rows // steps

    def fetch(req, carry):
        for at in range(list_len):
            pltpu.make_async_copy(
                pool.at[table[req, at]], pages.at[req, at], page_sem.at[req]
            ).start()
        return carry

    lax.fori_loop(0, local_reqs, fetch, 0)
    token = lax.broadcasted_iota(jnp.int32, (q_rows, cache_len), 1)
    column = lax.broadcasted_iota(jnp.int32, (q_rows, recent), 1)
    moment = lax.broadcasted_iota(jnp.int32, (q_rows, recent), 0) // group_width

    def one_request(req):
        pltpu.make_async_copy(
            pool.at[pl.ds(0, list_len)], pages.at[req], page_sem.at[req]
        ).wait()
        slot = slots[req]
        valid = token < lengths[req]
        base = kv_heads * q_rows
        new_keys = slabs[slot, base : base + recent, :]
        new_values = slabs[slot, base + recent : base + 2 * recent, :]
        for head in range(kv_heads):
            cols = slice(head * HEAD_SIZE, (head + 1) * HEAD_SIZE)
            query = slabs[slot, head * q_rows : (head + 1) * q_rows, :]
            keys = pages[req, :, 0, :, cols].reshape(cache_len, HEAD_SIZE)
            values = pages[req, :, 1, :, cols].reshape(cache_len, HEAD_SIZE)
            contract = (((1,), (1,)), ((), ()))
            old = lax.dot_general(query, keys, contract, preferred_element_type=jnp.float32)
            new = lax.dot_general(query, new_keys, contract, preferred_element_type=jnp.float32)
            seen = (column >= head * steps) & (column <= head * steps + moment)
            old = jnp.where(valid, old * scale, -jnp.inf)
            new = jnp.where(seen, new * scale, -jnp.inf)
            top = jnp.maximum(
                jnp.max(old, axis=1, keepdims=True), jnp.max(new, axis=1, keepdims=True)
            )
            old = jnp.exp(old - top)
            new = jnp.exp(new - top)
            total = jnp.sum(old, axis=1, keepdims=True) + jnp.sum(new, axis=1, keepdims=True)
            mixed = jnp.dot(
                old.astype(jnp.bfloat16), values, preferred_element_type=jnp.float32
            ) + jnp.dot(new.astype(jnp.bfloat16), new_values, preferred_element_type=jnp.float32)
            out[slot, head * q_rows : (head + 1) * q_rows, :] = (mixed / total).astype(jnp.bfloat16)

    unroll = 4

    def some_requests(at, carry):
        for offset in range(unroll):
            one_request(at * unroll + offset)
        return carry

    lax.fori_loop(0, local_reqs // unroll, some_requests, 0)


def attention(slabs, pool, table, lengths, slots, kv_heads, q_rows, steps):
    local_reqs, list_len = table.shape
    smem = pl.BlockSpec(memory_space=pltpu.SMEM)
    return pl.pallas_call(
        functools.partial(attention_kernel, kv_heads, q_rows, steps),
        out_shape=jax.ShapeDtypeStruct((local_reqs, kv_heads * q_rows, HEAD_SIZE), jnp.bfloat16),
        in_specs=[smem, smem, smem, VMEM, ANY],
        out_specs=VMEM,
        scratch_shapes=[
            pltpu.VMEM((local_reqs, list_len) + pool.shape[1:], pool.dtype),
            pltpu.SemaphoreType.DMA((local_reqs,)),
        ],
        compiler_params=pltpu.CompilerParams(vmem_limit_bytes=VMEM_LIMIT),
    )(table, lengths, slots, slabs, pool)


def scan_chunk_of(block_width):
    return min(512, block_width)


def back_kernel(
    ob,
    conv_out,
    normed,
    coefs,
    place_back,
    dt_proj,
    dt_bias,
    a_log,
    skip_d,
    state,
    o_out,
    y_out,
    held,
    rate_w,
    rates,
    drives,
    readings,
    ready,
    o_send,
    o_recv,
    y_send,
    y_recv,
    local_sem,
    chunk_sem,
):
    n = lax.axis_size("req")
    me = lax.axis_index("req")
    splits, _, rows = place_back.shape
    local_reqs, state_size, channels = state.shape
    steps = rows // local_reqs
    block_width = channels // splits
    chunk = scan_chunk_of(block_width)
    chunks = block_width // chunk
    for w_at in range(chunks):
        for split in range(splits):
            at = split * chunks + w_at
            cols = pl.ds(at * chunk, chunk)
            pltpu.make_async_copy(dt_proj.at[:, cols], rate_w.at[:, cols], chunk_sem.at[0, at]).start()
            pltpu.make_async_copy(
                state.at[:, :, cols], held.at[:, :, cols], chunk_sem.at[1, at]
            ).start()
    own_o = pltpu.make_async_copy(ob.at[me], o_out.at[me], local_sem.at[0])
    own_o.start()
    greet(("req",))
    o_copies = []
    for step in range(1, n):
        peer = lax.rem(me + step, n)
        o_copies.append(
            remote(ob.at[peer], o_out.at[me], o_send.at[step], o_recv.at[step], "req", peer)
        )
        o_copies[-1].start()

    def one_chunk(w_at, carry):
        inner = pl.ds(pl.multiple_of(w_at * chunk, chunk), chunk)
        blocks = jnp.zeros((n * BLOCK_ROWS, chunk), jnp.float32)
        for split in range(splits):
            at = split * chunks + w_at
            outer = pl.ds(pl.multiple_of(at * chunk, chunk), chunk)
            pltpu.make_async_copy(
                dt_proj.at[:, outer], rate_w.at[:, outer], chunk_sem.at[0, at]
            ).wait()
            raw = (
                jnp.dot(normed[...], rate_w[:, outer], preferred_element_type=jnp.float32)
                + dt_bias[:, outer]
            )
            rate = jnp.maximum(raw, 0.0) + jnp.log1p(jnp.exp(-jnp.abs(raw)))
            inputs = conv_out[:, outer].astype(jnp.float32)
            rates[...] = rate
            drives[...] = rate * inputs
            decay = jnp.exp(a_log[:, outer]) * (-LOG2E)
            pltpu.make_async_copy(
                state.at[:, :, outer], held.at[:, :, outer], chunk_sem.at[1, at]
            ).wait()

            def one_request(req, inner_carry):
                hidden = held[req, :, outer]
                pair = coefs[req]
                for t in range(steps):
                    row = pl.ds(t * local_reqs + req, 1)
                    hidden = jnp.exp2(rates[row, :] * decay) * hidden + drives[row, :] * pair[:, t : t + 1]
                    readings[row, :] = jnp.sum(
                        hidden * pair[:, steps + t : steps + t + 1], axis=0, keepdims=True
                    )
                return inner_carry

            lax.fori_loop(0, local_reqs, one_request, 0)
            reading = (readings[...] + skip_d[:, outer] * inputs).astype(jnp.bfloat16)
            blocks = blocks + jnp.dot(
                place_back[split], reading, preferred_element_type=jnp.float32
            )
        ready[:, :, inner] = blocks.astype(jnp.bfloat16).reshape(n, BLOCK_ROWS, chunk)
        for step in range(1, n):
            peer = lax.rem(me + step, n)
            remote(
                ready.at[peer, :, inner],
                y_out.at[me, :, inner],
                y_send.at[step],
                y_recv.at[step],
                "req",
                peer,
            ).start()
        return carry

    lax.fori_loop(0, chunks, one_chunk, 0)
    own_y = pltpu.make_async_copy(ready.at[me], y_out.at[me], local_sem.at[1])
    own_y.start()
    own_o.wait()
    for copy in o_copies:
        copy.wait()
    for step in range(1, n):
        peer = lax.rem(me + step, n)
        remote(
            ready.at[peer], y_out.at[me], y_send.at[step], y_recv.at[step], "req", peer
        ).wait()
    own_y.wait()


def back(ob, conv_out, normed, coefs, place_back, dt_proj, dt_bias, a_log, skip_d, state):
    n = ob.shape[0]
    splits, block_total, rows = place_back.shape
    channels = state.shape[2]
    block_width = channels // splits
    chunk = scan_chunk_of(block_width)
    dma = pltpu.SemaphoreType.DMA
    blocks = (n, BLOCK_ROWS, block_width)
    return pl.pallas_call(
        back_kernel,
        out_shape=(
            jax.ShapeDtypeStruct(ob.shape, ob.dtype),
            jax.ShapeDtypeStruct(blocks, jnp.bfloat16),
        ),
        in_specs=[ANY, VMEM, VMEM, VMEM, VMEM, ANY, VMEM, VMEM, VMEM, ANY],
        out_specs=(ANY, ANY),
        scratch_shapes=[
            pltpu.VMEM(state.shape, state.dtype),
            pltpu.VMEM(dt_proj.shape, dt_proj.dtype),
            pltpu.VMEM((rows, chunk), jnp.float32),
            pltpu.VMEM((rows, chunk), jnp.float32),
            pltpu.VMEM((rows, chunk), jnp.float32),
            pltpu.VMEM(blocks, jnp.bfloat16),
            dma((n,)),
            dma((n,)),
            dma((n,)),
            dma((n,)),
            dma((2,)),
            dma((2, channels // chunk)),
        ],
        compiler_params=pltpu.CompilerParams(
            collective_id=1, has_side_effects=True, vmem_limit_bytes=VMEM_LIMIT
        ),
    )(ob, conv_out, normed, coefs, place_back, dt_proj, dt_bias, a_log, skip_d, state)


def per_device(
    queries,
    new_kv,
    prefill_page_pool,
    page_table,
    prompt_len,
    dest_device,
    ssm_state,
    conv_state,
    mamba_x,
    mamba_z,
    conv_weight,
    conv_bias,
    x_proj,
    dt_gain,
    dt_proj,
    dt_bias,
    a_log,
    skip_d,
):
    n = lax.axis_size("req")
    local_reqs = dest_device.shape[0]
    steps = queries.shape[0]
    channels = mamba_x.shape[2]
    kv_heads = prefill_page_pool.shape[3] // HEAD_SIZE
    group_width = queries.shape[2] // HEAD_SIZE // kv_heads
    q_rows = steps * group_width
    state_size = a_log.shape[0]
    share = local_reqs // n
    splits = BLOCK_ROWS // (steps * share)
    block_width = channels // splits
    index = jnp.arange(local_reqs, dtype=jnp.int32)
    same = dest_device[:, None] == dest_device[None, :]
    rank = jnp.sum((same & (index[None, :] < index[:, None])).astype(jnp.int32), axis=1)
    slots = dest_device * share + rank
    times = jnp.arange(steps, dtype=jnp.int32)
    split_ids = jnp.arange(splits, dtype=jnp.int32)
    block_row = dest_device * BLOCK_ROWS + rank * splits
    block_row = (
        block_row[None, None, :]
        + times[None, :, None] * (share * splits)
        + split_ids[:, None, None]
    ).reshape(splits, steps * local_reqs)
    block_ids = jnp.arange(n * BLOCK_ROWS, dtype=jnp.int32)
    place = (block_row[:, :, None] == block_ids[None, None, :]).astype(jnp.bfloat16)
    place_back = (block_row[:, None, :] == block_ids[None, :, None]).astype(jnp.bfloat16)

    xb = jnp.transpose(
        mamba_x.reshape(steps, n, share, channels), (1, 0, 2, 3)
    ).reshape(n, BLOCK_ROWS, block_width)
    q_part = jnp.transpose(
        queries.reshape(steps, local_reqs, kv_heads, group_width, HEAD_SIZE), (1, 2, 0, 3, 4)
    ).reshape(local_reqs, kv_heads * q_rows, HEAD_SIZE)
    kv_part = jnp.transpose(
        new_kv.reshape(steps, local_reqs, 2, kv_heads, HEAD_SIZE), (1, 2, 3, 0, 4)
    ).reshape(local_reqs, 2 * kv_heads * steps, HEAD_SIZE)
    slabs = jnp.concatenate([q_part, kv_part], axis=1)
    slab_rows = slabs.shape[1]
    conv_out, normed, coefs, slabs = front(
        xb,
        slabs.reshape(n, share * slab_rows, HEAD_SIZE),
        jnp.transpose(conv_state, (1, 0, 2)),
        place,
        conv_weight,
        conv_bias[None],
        x_proj,
        dt_gain[None],
    )
    ob = attention(
        slabs.reshape(local_reqs, slab_rows, HEAD_SIZE),
        prefill_page_pool,
        page_table,
        prompt_len,
        slots,
        kv_heads,
        q_rows,
        steps,
    )
    coefs = jnp.transpose(
        coefs[:, : 2 * state_size].reshape(steps, local_reqs, 2, state_size), (1, 3, 2, 0)
    ).reshape(local_reqs, state_size, 2 * steps)
    o_back, y_back = back(
        ob.reshape(n, share * kv_heads * q_rows, HEAD_SIZE),
        conv_out,
        normed,
        coefs,
        place_back,
        dt_proj,
        dt_bias[None],
        a_log,
        skip_d[None],
        ssm_state,
    )
    attn_out = jnp.transpose(
        o_back.reshape(local_reqs, kv_heads, steps, group_width, HEAD_SIZE), (2, 0, 1, 3, 4)
    ).reshape(queries.shape)
    reading = jnp.transpose(
        y_back.reshape(n, steps, share, channels), (1, 0, 2, 3)
    ).reshape(mamba_x.shape)
    gate_values = jax.nn.silu(mamba_z.astype(jnp.float32))
    mamba_out = (reading.astype(jnp.float32) * gate_values).astype(jnp.bfloat16)
    return (attn_out, mamba_out)


def solution(mesh):
    return jax.shard_map(
        per_device,
        mesh=mesh,
        in_specs=(
            P(None, "req", "tp"),
            P(None, "req", None, "tp"),
            P("req", None, None, "tp"),
            P("req", None),
            P("req"),
            P("req"),
            P("req", None, "tp"),
            P("req", None, "tp"),
            P(None, "req", "tp"),
            P(None, "req", "tp"),
            P(None, "tp"),
            P("tp"),
            P("tp", None),
            P(),
            P(None, "tp"),
            P("tp"),
            P(None, "tp"),
            P("tp"),
        ),
        out_specs=(P(None, "req", "tp"), P(None, "req", "tp")),
        check_vma=False,
    )
```

```python
import functools
import math

import jax
import jax.numpy as jnp
from jax import lax
from jax.experimental import pallas as pl
from jax.experimental.pallas import tpu as pltpu
from jax.sharding import PartitionSpec as P

HEAD_SIZE = 128
BLOCK_ROWS = 16
EPSILON = 1e-06
LOG2E = 1.4426950408889634
VMEM_LIMIT = 56 * 1024 * 1024
MESH = pl.DeviceIdType.MESH
ANY = pl.BlockSpec(memory_space=pl.ANY)
VMEM = pl.BlockSpec(memory_space=pltpu.VMEM)


def greet(axes):
    barrier = pltpu.get_barrier_semaphore()
    total = 0
    for name in axes:
        size = lax.axis_size(name)
        me = lax.axis_index(name)
        for step in range(1, size):
            pl.semaphore_signal(
                barrier, inc=1, device_id={name: lax.rem(me + step, size)}, device_id_type=MESH
            )
        total += size - 1
    pl.semaphore_wait(barrier, total)


def remote(src, dst, send_sem, recv_sem, axis, peer):
    return pltpu.make_async_remote_copy(
        src_ref=src,
        dst_ref=dst,
        send_sem=send_sem,
        recv_sem=recv_sem,
        device_id={axis: peer},
        device_id_type=MESH,
    )


def bring(sems, *pairs):
    copies = [
        pltpu.make_async_copy(src, dst, sems.at[at]) for at, (src, dst) in enumerate(pairs)
    ]
    for copy in copies:
        copy.start()
    return copies


def like(value):
    return pltpu.VMEM(value.shape, value.dtype)


def front_kernel(
    xb,
    qb,
    conv_rows_far,
    place_far,
    conv_weight_far,
    conv_bias_far,
    x_proj,
    dt_gain_far,
    conv_out,
    normed,
    coefs,
    q_out,
    conv_rows,
    place,
    conv_weight,
    conv_bias,
    dt_gain,
    load_sem,
    x_in,
    proj_w,
    part,
    gathered,
    x_send,
    x_recv,
    q_send,
    q_recv,
    local_sem,
    rs_send,
    rs_recv,
    ag_send,
    ag_recv,
):
    n = lax.axis_size("req")
    width = lax.axis_size("tp")
    me = lax.axis_index("req")
    lane = lax.axis_index("tp")
    splits, rows, _ = place.shape
    block_width = xb.shape[2]
    local_reqs = conv_rows.shape[1]
    steps = rows // local_reqs
    taps = conv_weight.shape[0]
    rank_width = dt_gain.shape[1]
    proj_width = x_proj.shape[0]
    piece = rows // width
    loads = bring(
        load_sem,
        (conv_rows_far, conv_rows),
        (place_far, place),
        (conv_weight_far, conv_weight),
        (conv_bias_far, conv_bias),
        (dt_gain_far, dt_gain),
    )
    weights_copy = pltpu.make_async_copy(x_proj, proj_w, local_sem.at[0])
    weights_copy.start()
    own_x = pltpu.make_async_copy(xb.at[me], x_in.at[me], local_sem.at[1])
    own_x.start()
    own_q = pltpu.make_async_copy(qb.at[me], q_out.at[me], local_sem.at[2])
    own_q.start()
    greet(("req", "tp"))
    x_copies, q_copies = [], []
    for step in range(1, n):
        peer = lax.rem(me + step, n)
        x_copies.append(
            remote(xb.at[peer], x_in.at[me], x_send.at[step], x_recv.at[step], "req", peer)
        )
        x_copies[-1].start()
    part[...] = jnp.zeros_like(part)
    for copy in loads:
        copy.wait()
    own_x.wait()
    weights_copy.wait()
    for copy in x_copies:
        copy.wait()
    for step in range(1, n):
        peer = lax.rem(me + step, n)
        q_copies.append(
            remote(qb.at[peer], q_out.at[me], q_send.at[step], q_recv.at[step], "req", peer)
        )
        q_copies[-1].start()
    chunk = min(512, block_width)
    for split in range(splits):

        def one_chunk(at, carry):
            inner = pl.ds(pl.multiple_of(at * chunk, chunk), chunk)
            outer = pl.ds(pl.multiple_of(split * block_width + at * chunk, chunk), chunk)
            block = x_in[:, :, inner].reshape(n * BLOCK_ROWS, chunk)
            fresh = jnp.dot(place[split], block, preferred_element_type=jnp.float32)
            window = [conv_rows[row, :, outer].astype(jnp.float32) for row in range(taps - 1)]
            window += [fresh[t * local_reqs : (t + 1) * local_reqs] for t in range(steps)]
            for t in range(steps):
                total = conv_bias[:, outer] + sum(
                    conv_weight[tap : tap + 1, outer] * window[t + tap] for tap in range(taps)
                )
                active = total / (1.0 + jnp.exp(-total))
                conv_out[t * local_reqs : (t + 1) * local_reqs, outer] = active.astype(jnp.bfloat16)
            part[:, :proj_width] += lax.dot_general(
                conv_out[:, outer],
                proj_w[:, outer],
                (((1,), (1,)), ((), ())),
                preferred_element_type=jnp.float32,
            )
            return carry

        lax.fori_loop(0, block_width // chunk, one_chunk, 0)
    copies = []
    for step in range(1, width):
        peer = lax.rem(lane + step, width)
        copies.append(
            remote(
                part.at[pl.ds(pl.multiple_of(peer * piece, piece), piece)],
                gathered.at[step],
                rs_send.at[step],
                rs_recv.at[step],
                "tp",
                peer,
            )
        )
        copies[-1].start()
    mine = pl.ds(pl.multiple_of(lane * piece, piece), piece)
    gathered[0] = part[mine, :]
    for copy in copies:
        copy.wait()
    summed = gathered[0]
    for step in range(1, width):
        summed = summed + gathered[step]
    dt_low = summed[:, :rank_width]
    scale = lax.rsqrt(jnp.mean(dt_low * dt_low, axis=-1, keepdims=True) + EPSILON)
    normed[mine, :] = (dt_low * scale * dt_gain[...]).astype(jnp.bfloat16)
    coefs[mine, :] = summed[:, rank_width:]
    copies = []
    for step in range(1, width):
        peer = lax.rem(lane + step, width)
        for at, ref in enumerate((normed, coefs)):
            copies.append(
                remote(
                    ref.at[mine], ref.at[mine], ag_send.at[at, step], ag_recv.at[at, step], "tp", peer
                )
            )
            copies[-1].start()
    for copy in copies:
        copy.wait()
    own_q.wait()
    for copy in q_copies:
        copy.wait()


def front(xb, qb, conv_rows, place, conv_weight, conv_bias, x_proj, dt_gain):
    n = xb.shape[0]
    width = lax.axis_size("tp")
    rows = place.shape[1]
    channels = conv_weight.shape[1]
    rank_width = dt_gain.shape[1]
    wide = rank_width + 128
    dma = pltpu.SemaphoreType.DMA
    return pl.pallas_call(
        front_kernel,
        out_shape=(
            jax.ShapeDtypeStruct((rows, channels), jnp.bfloat16),
            jax.ShapeDtypeStruct((rows, rank_width), jnp.bfloat16),
            jax.ShapeDtypeStruct((rows, 128), jnp.float32),
            jax.ShapeDtypeStruct(qb.shape, qb.dtype),
        ),
        in_specs=[ANY] * 8,
        out_specs=(VMEM, VMEM, VMEM, ANY),
        scratch_shapes=[
            like(conv_rows),
            like(place),
            like(conv_weight),
            like(conv_bias),
            like(dt_gain),
            dma((5,)),
            pltpu.VMEM(xb.shape, xb.dtype),
            pltpu.VMEM(x_proj.shape, x_proj.dtype),
            pltpu.VMEM((rows, wide), jnp.float32),
            pltpu.VMEM((width, rows // width, wide), jnp.float32),
            dma((n,)),
            dma((n,)),
            dma((n,)),
            dma((n,)),
            dma((3,)),
            dma((width,)),
            dma((width,)),
            dma((2, width)),
            dma((2, width)),
        ],
        compiler_params=pltpu.CompilerParams(
            collective_id=0, has_side_effects=True, vmem_limit_bytes=VMEM_LIMIT
        ),
    )(xb, qb, conv_rows, place, conv_weight, conv_bias, x_proj, dt_gain)


def attention_kernel(kv_heads, q_rows, steps, table, lengths, slots, slabs, pool, out):
    local_reqs, list_len = table.shape
    cache_len = list_len * pool.shape[2]
    scale = 1.0 / math.sqrt(HEAD_SIZE)
    recent = kv_heads * steps
    all_rows = kv_heads * q_rows
    group_width = q_rows // steps
    token = lax.broadcasted_iota(jnp.int32, (all_rows, cache_len), 1)
    column = lax.broadcasted_iota(jnp.int32, (all_rows, recent), 1)
    row = lax.broadcasted_iota(jnp.int32, (all_rows, recent), 0)
    row_head = row // q_rows
    row_moment = (row - row_head * q_rows) // group_width
    seen = (column >= row_head * steps) & (column <= row_head * steps + row_moment)
    contract = (((1,), (1,)), ((), ()))
    together = 4

    def some_requests(at, carry):
        reqs = [at * together + offset for offset in range(together)]
        rows = [slots[req] for req in reqs]
        scores, fresh = [], []
        for req, slot in zip(reqs, rows):
            keys = jnp.concatenate([pool[table[req, i], 0] for i in range(list_len)], axis=0)
            parts = [
                lax.dot_general(
                    slabs[slot, head * q_rows : (head + 1) * q_rows, :],
                    keys[:, head * HEAD_SIZE : (head + 1) * HEAD_SIZE],
                    contract,
                    preferred_element_type=jnp.float32,
                )
                for head in range(kv_heads)
            ]
            scores.append(jnp.concatenate(parts, axis=0))
            fresh.append(
                lax.dot_general(
                    slabs[slot, :all_rows, :],
                    slabs[slot, all_rows : all_rows + recent, :],
                    contract,
                    preferred_element_type=jnp.float32,
                )
            )
        weights = []
        for req, old, new in zip(reqs, scores, fresh):
            old = jnp.where(token < lengths[req], old * scale, -jnp.inf)
            new = jnp.where(seen, new * scale, -jnp.inf)
            top = jnp.maximum(
                jnp.max(old, axis=1, keepdims=True), jnp.max(new, axis=1, keepdims=True)
            )
            old = jnp.exp(old - top)
            new = jnp.exp(new - top)
            total = jnp.sum(old, axis=1, keepdims=True) + jnp.sum(new, axis=1, keepdims=True)
            weights.append((old.astype(jnp.bfloat16), new.astype(jnp.bfloat16), 1.0 / total))
        for req, slot, (old, new, inverse) in zip(reqs, rows, weights):
            values = jnp.concatenate([pool[table[req, i], 1] for i in range(list_len)], axis=0)
            parts = [
                jnp.dot(
                    old[head * q_rows : (head + 1) * q_rows, :],
                    values[:, head * HEAD_SIZE : (head + 1) * HEAD_SIZE],
                    preferred_element_type=jnp.float32,
                )
                for head in range(kv_heads)
            ]
            mixed = jnp.concatenate(parts, axis=0) + jnp.dot(
                new,
                slabs[slot, all_rows + recent : all_rows + 2 * recent, :],
                preferred_element_type=jnp.float32,
            )
            out[slot] = (mixed * inverse).astype(jnp.bfloat16)
        return carry

    lax.fori_loop(0, local_reqs // together, some_requests, 0)


def attention(slabs, pool, table, lengths, slots, kv_heads, q_rows, steps):
    local_reqs = table.shape[0]
    smem = pl.BlockSpec(memory_space=pltpu.SMEM)
    return pl.pallas_call(
        functools.partial(attention_kernel, kv_heads, q_rows, steps),
        out_shape=jax.ShapeDtypeStruct((local_reqs, kv_heads * q_rows, HEAD_SIZE), jnp.bfloat16),
        in_specs=[smem, smem, smem, VMEM, VMEM],
        out_specs=VMEM,
        compiler_params=pltpu.CompilerParams(vmem_limit_bytes=VMEM_LIMIT),
    )(table, lengths, slots, slabs, pool)


def scan_chunk_of(block_width):
    return min(512, block_width)


def back_kernel(
    ob,
    conv_out_far,
    normed_far,
    coefs_far,
    place_back_far,
    dt_proj,
    dt_bias_far,
    a_log_far,
    skip_d_far,
    state,
    o_out,
    y_out,
    conv_out,
    normed,
    coefs,
    place_back,
    dt_bias,
    a_log,
    skip_d,
    load_sem,
    b_wide,
    c_wide,
    decay,
    held,
    rate_w,
    rates,
    drives,
    readings,
    ready,
    o_send,
    o_recv,
    y_send,
    y_recv,
    local_sem,
    chunk_sem,
    state_sem,
):
    n = lax.axis_size("req")
    me = lax.axis_index("req")
    splits, _, rows = place_back.shape
    state_size, channels = a_log.shape
    local_reqs = state.shape[0] // state_size
    steps = rows // local_reqs
    block_width = channels // splits
    chunk = scan_chunk_of(block_width)
    chunks = block_width // chunk
    tiles = chunk // 128
    loads = bring(
        load_sem,
        (conv_out_far, conv_out),
        (normed_far, normed),
        (coefs_far, coefs),
        (place_back_far, place_back),
        (dt_bias_far, dt_bias),
        (a_log_far, a_log),
        (skip_d_far, skip_d),
    )

    def state_copy(tile):
        lanes = pl.ds(pl.multiple_of(tile * 128, 128), 128)
        return pltpu.make_async_copy(state.at[:, lanes], held.at[tile], state_sem.at[tile])

    for w_at in range(chunks):
        for split in range(splits):
            at = split * chunks + w_at
            cols = pl.ds(at * chunk, chunk)
            pltpu.make_async_copy(dt_proj.at[:, cols], rate_w.at[:, cols], chunk_sem.at[at]).start()
            for tile in range(tiles):
                state_copy(at * tiles + tile).start()
    own_o = pltpu.make_async_copy(ob.at[me], o_out.at[me], local_sem.at[0])
    own_o.start()
    greet(("req",))
    o_copies = []
    for step in range(1, n):
        peer = lax.rem(me + step, n)
        o_copies.append(
            remote(ob.at[peer], o_out.at[me], o_send.at[step], o_recv.at[step], "req", peer)
        )
        o_copies[-1].start()

    for copy in loads:
        copy.wait()
    for t in range(steps):
        at_rows = slice(t * local_reqs, (t + 1) * local_reqs)
        for entry in range(state_size):
            for wide, column in ((b_wide, entry), (c_wide, state_size + entry)):
                wide[t, entry] = jnp.broadcast_to(
                    coefs[at_rows, column : column + 1], (local_reqs, 128)
                )
    groups = local_reqs // 8

    def one_chunk(w_at, carry):
        inner = pl.ds(pl.multiple_of(w_at * chunk, chunk), chunk)
        blocks = jnp.zeros((n * BLOCK_ROWS, chunk), jnp.float32)
        for split in range(splits):
            at = split * chunks + w_at
            outer = pl.ds(pl.multiple_of(at * chunk, chunk), chunk)
            pltpu.make_async_copy(
                dt_proj.at[:, outer], rate_w.at[:, outer], chunk_sem.at[at]
            ).wait()
            raw = (
                jnp.dot(normed[...], rate_w[:, outer], preferred_element_type=jnp.float32)
                + dt_bias[:, outer]
            )
            rate = jnp.maximum(raw, 0.0) + jnp.log1p(jnp.exp(-jnp.abs(raw)))
            inputs = conv_out[:, outer].astype(jnp.float32)
            rates[...] = rate
            drives[...] = rate * inputs
            decay[...] = jnp.exp(a_log[:, outer]) * (-LOG2E)
            for tile in range(tiles):
                state_copy(at * tiles + tile).wait()

            def one_tile(cell, inner_carry):
                tile = cell // groups
                first = pl.multiple_of((cell - tile * groups) * 8, 8)
                lanes = pl.ds(pl.multiple_of(tile * 128, 128), 128)
                rows_at = [pl.ds(pl.multiple_of(t * local_reqs + first, 8), 8) for t in range(steps)]
                rate_t = [rates[rows_at[t], lanes] for t in range(steps)]
                drive_t = [drives[rows_at[t], lanes] for t in range(steps)]
                sums = [jnp.zeros((8, 128), jnp.float32) for _ in range(steps)]
                for entry in range(state_size):
                    hidden = held[
                        at * tiles + tile, pl.ds(first * state_size + entry, 8, stride=state_size), :
                    ]
                    slope = decay[entry : entry + 1, lanes]
                    for t in range(steps):
                        hidden = (
                            jnp.exp2(rate_t[t] * slope) * hidden
                            + drive_t[t] * b_wide[t, entry, pl.ds(first, 8), :]
                        )
                        sums[t] = sums[t] + hidden * c_wide[t, entry, pl.ds(first, 8), :]
                for t in range(steps):
                    readings[rows_at[t], lanes] = sums[t]
                return inner_carry

            lax.fori_loop(0, tiles * groups, one_tile, 0)
            reading = (readings[...] + skip_d[:, outer] * inputs).astype(jnp.bfloat16)
            blocks = blocks + jnp.dot(
                place_back[split], reading, preferred_element_type=jnp.float32
            )
        ready[:, :, inner] = blocks.astype(jnp.bfloat16).reshape(n, BLOCK_ROWS, chunk)
        for step in range(1, n):
            peer = lax.rem(me + step, n)
            remote(
                ready.at[peer, :, inner],
                y_out.at[me, :, inner],
                y_send.at[step],
                y_recv.at[step],
                "req",
                peer,
            ).start()
        return carry

    lax.fori_loop(0, chunks, one_chunk, 0)
    own_y = pltpu.make_async_copy(ready.at[me], y_out.at[me], local_sem.at[1])
    own_y.start()
    own_o.wait()
    for copy in o_copies:
        copy.wait()
    for step in range(1, n):
        peer = lax.rem(me + step, n)
        remote(
            ready.at[peer], y_out.at[me], y_send.at[step], y_recv.at[step], "req", peer
        ).wait()
    own_y.wait()


def back(ob, conv_out, normed, coefs, place_back, dt_proj, dt_bias, a_log, skip_d, state):
    n = ob.shape[0]
    splits, block_total, rows = place_back.shape
    channels = state.shape[1]
    state_size = a_log.shape[0]
    local_reqs = state.shape[0] // state_size
    steps = rows // local_reqs
    block_width = channels // splits
    chunk = scan_chunk_of(block_width)
    dma = pltpu.SemaphoreType.DMA
    blocks = (n, BLOCK_ROWS, block_width)
    return pl.pallas_call(
        back_kernel,
        out_shape=(
            jax.ShapeDtypeStruct(ob.shape, ob.dtype),
            jax.ShapeDtypeStruct(blocks, jnp.bfloat16),
        ),
        in_specs=[ANY] * 10,
        out_specs=(ANY, ANY),
        scratch_shapes=[
            like(conv_out),
            like(normed),
            like(coefs),
            like(place_back),
            like(dt_bias),
            like(a_log),
            like(skip_d),
            dma((7,)),
            pltpu.VMEM((steps, state_size, local_reqs, 128), jnp.float32),
            pltpu.VMEM((steps, state_size, local_reqs, 128), jnp.float32),
            pltpu.VMEM((state_size, chunk), jnp.float32),
            pltpu.VMEM((channels // 128, local_reqs * state_size, 128), jnp.float32),
            pltpu.VMEM(dt_proj.shape, dt_proj.dtype),
            pltpu.VMEM((rows, chunk), jnp.float32),
            pltpu.VMEM((rows, chunk), jnp.float32),
            pltpu.VMEM((rows, chunk), jnp.float32),
            pltpu.VMEM(blocks, jnp.bfloat16),
            dma((n,)),
            dma((n,)),
            dma((n,)),
            dma((n,)),
            dma((2,)),
            dma((channels // chunk,)),
            dma((channels // 128,)),
        ],
        compiler_params=pltpu.CompilerParams(
            collective_id=1, has_side_effects=True, vmem_limit_bytes=VMEM_LIMIT
        ),
    )(ob, conv_out, normed, coefs, place_back, dt_proj, dt_bias, a_log, skip_d, state)


def per_device(
    queries,
    new_kv,
    prefill_page_pool,
    page_table,
    prompt_len,
    dest_device,
    ssm_state,
    conv_state,
    mamba_x,
    mamba_z,
    conv_weight,
    conv_bias,
    x_proj,
    dt_gain,
    dt_proj,
    dt_bias,
    a_log,
    skip_d,
):
    n = lax.axis_size("req")
    local_reqs = dest_device.shape[0]
    steps = queries.shape[0]
    channels = mamba_x.shape[2]
    kv_heads = prefill_page_pool.shape[3] // HEAD_SIZE
    group_width = queries.shape[2] // HEAD_SIZE // kv_heads
    q_rows = steps * group_width
    state_size = a_log.shape[0]
    share = local_reqs // n
    splits = BLOCK_ROWS // (steps * share)
    block_width = channels // splits
    index = jnp.arange(local_reqs, dtype=jnp.int32)
    same = dest_device[:, None] == dest_device[None, :]
    rank = jnp.sum((same & (index[None, :] < index[:, None])).astype(jnp.int32), axis=1)
    slots = dest_device * share + rank
    times = jnp.arange(steps, dtype=jnp.int32)
    split_ids = jnp.arange(splits, dtype=jnp.int32)
    block_row = dest_device * BLOCK_ROWS + rank * splits
    block_row = (
        block_row[None, None, :]
        + times[None, :, None] * (share * splits)
        + split_ids[:, None, None]
    ).reshape(splits, steps * local_reqs)
    block_ids = jnp.arange(n * BLOCK_ROWS, dtype=jnp.int32)
    place = (block_row[:, :, None] == block_ids[None, None, :]).astype(jnp.bfloat16)
    place_back = (block_row[:, None, :] == block_ids[None, :, None]).astype(jnp.bfloat16)

    xb = jnp.transpose(
        mamba_x.reshape(steps, n, share, channels), (1, 0, 2, 3)
    ).reshape(n, BLOCK_ROWS, block_width)
    q_part = jnp.transpose(
        queries.reshape(steps, local_reqs, kv_heads, group_width, HEAD_SIZE), (1, 2, 0, 3, 4)
    ).reshape(local_reqs, kv_heads * q_rows, HEAD_SIZE)
    kv_part = jnp.transpose(
        new_kv.reshape(steps, local_reqs, 2, kv_heads, HEAD_SIZE), (1, 2, 3, 0, 4)
    ).reshape(local_reqs, 2 * kv_heads * steps, HEAD_SIZE)
    slabs = jnp.concatenate([q_part, kv_part], axis=1)
    slab_rows = slabs.shape[1]
    conv_out, normed, coefs, slabs = front(
        xb,
        slabs.reshape(n, share * slab_rows, HEAD_SIZE),
        jnp.transpose(conv_state, (1, 0, 2)),
        place,
        conv_weight,
        conv_bias[None],
        x_proj.T,
        dt_gain[None],
    )
    ob = attention(
        slabs.reshape(local_reqs, slab_rows, HEAD_SIZE),
        prefill_page_pool,
        page_table,
        prompt_len,
        slots,
        kv_heads,
        q_rows,
        steps,
    )
    o_back, y_back = back(
        ob.reshape(n, share * kv_heads * q_rows, HEAD_SIZE),
        conv_out,
        normed,
        coefs,
        place_back,
        dt_proj,
        dt_bias[None],
        a_log,
        skip_d[None],
        ssm_state.reshape(local_reqs * state_size, channels),
    )
    attn_out = jnp.transpose(
        o_back.reshape(local_reqs, kv_heads, steps, group_width, HEAD_SIZE), (2, 0, 1, 3, 4)
    ).reshape(queries.shape)
    reading = jnp.transpose(
        y_back.reshape(n, steps, share, channels), (1, 0, 2, 3)
    ).reshape(mamba_x.shape)
    gate_values = jax.nn.silu(mamba_z.astype(jnp.float32))
    mamba_out = (reading.astype(jnp.float32) * gate_values).astype(jnp.bfloat16)
    return (attn_out, mamba_out)


def solution(mesh):
    return jax.shard_map(
        per_device,
        mesh=mesh,
        in_specs=(
            P(None, "req", "tp"),
            P(None, "req", None, "tp"),
            P("req", None, None, "tp"),
            P("req", None),
            P("req"),
            P("req"),
            P("req", None, "tp"),
            P("req", None, "tp"),
            P(None, "req", "tp"),
            P(None, "req", "tp"),
            P(None, "tp"),
            P("tp"),
            P("tp", None),
            P(),
            P(None, "tp"),
            P("tp"),
            P(None, "tp"),
            P("tp"),
        ),
        out_specs=(P(None, "req", "tp"), P(None, "req", "tp")),
        check_vma=False,
    )
```

```python
import functools
import math

import jax
import jax.numpy as jnp
from jax import lax
from jax.experimental import pallas as pl
from jax.experimental.pallas import tpu as pltpu
from jax.sharding import PartitionSpec as P

HEAD_SIZE = 128
BLOCK_ROWS = 16
X_PARTS = 2
EPSILON = 1e-06
LOG2E = 1.4426950408889634
VMEM_LIMIT = 56 * 1024 * 1024
MESH = pl.DeviceIdType.MESH
ANY = pl.BlockSpec(memory_space=pl.ANY)
VMEM = pl.BlockSpec(memory_space=pltpu.VMEM)


def greet(axes):
    barrier = pltpu.get_barrier_semaphore()
    total = 0
    for name in axes:
        size = lax.axis_size(name)
        me = lax.axis_index(name)
        for step in range(1, size):
            pl.semaphore_signal(
                barrier, inc=1, device_id={name: lax.rem(me + step, size)}, device_id_type=MESH
            )
        total += size - 1
    pl.semaphore_wait(barrier, total)


def remote(src, dst, send_sem, recv_sem, axis, peer):
    return pltpu.make_async_remote_copy(
        src_ref=src,
        dst_ref=dst,
        send_sem=send_sem,
        recv_sem=recv_sem,
        device_id={axis: peer},
        device_id_type=MESH,
    )


def bring(sems, *pairs):
    copies = [
        pltpu.make_async_copy(src, dst, sems.at[at]) for at, (src, dst) in enumerate(pairs)
    ]
    for copy in copies:
        copy.start()
    return copies


def like(value):
    return pltpu.VMEM(value.shape, value.dtype)


def decode_kernel(
    kv_heads,
    q_rows,
    steps,
    table,
    lengths,
    order,
    qb,
    xb,
    pool_far,
    conv_rows_far,
    place_far,
    place_back_far,
    conv_weight_far,
    conv_bias_far,
    x_proj,
    dt_gain_far,
    dt_proj,
    dt_bias_far,
    a_log_far,
    skip_d_far,
    state,
    o_out,
    y_out,
    pool,
    conv_rows,
    place,
    place_back,
    conv_weight,
    conv_bias,
    dt_gain,
    dt_bias,
    a_log,
    skip_d,
    proj_w,
    load_sem,
    q_in,
    x_in,
    o_ready,
    conv_out,
    part,
    gathered,
    normed,
    coefs,
    b_wide,
    c_wide,
    decay,
    held,
    rate_w,
    rates,
    drives,
    readings,
    ready,
    q_send,
    q_recv,
    x_send,
    x_recv,
    o_send,
    o_recv,
    y_send,
    y_recv,
    local_sem,
    chunk_sem,
    state_sem,
    rs_send,
    rs_recv,
    ag_send,
    ag_recv,
):
    n = lax.axis_size("req")
    width = lax.axis_size("tp")
    me = lax.axis_index("req")
    lane = lax.axis_index("tp")
    splits, rows, _ = place.shape
    block_width = xb.shape[2]
    local_reqs, list_len = table.shape
    share = local_reqs // n
    state_size, channels = a_log.shape
    taps = conv_weight.shape[0]
    rank_width = dt_gain.shape[1]
    proj_width = x_proj.shape[0]
    piece = rows // width
    half = block_width // X_PARTS
    chunk = min(512, half)
    span = scan_chunk_of(block_width)
    chunks = block_width // span
    spans = chunks
    tiles = span // 128
    mine_rows = pl.ds(me * share, share)
    own_q = pltpu.make_async_copy(qb.at[mine_rows], q_in.at[mine_rows], local_sem.at[0])
    own_q.start()
    own_x = pltpu.make_async_copy(xb.at[me], x_in.at[me], local_sem.at[1])
    own_x.start()
    loads = bring(
        load_sem,
        (pool_far, pool),
        (x_proj, proj_w),
        (conv_rows_far, conv_rows),
        (place_far, place),
        (place_back_far, place_back),
        (conv_weight_far, conv_weight),
        (conv_bias_far, conv_bias),
        (dt_gain_far, dt_gain),
        (dt_bias_far, dt_bias),
        (a_log_far, a_log),
        (skip_d_far, skip_d),
    )
    greet(("req", "tp"))
    peers = [lax.rem(me + step, n) for step in range(1, n)]
    q_copies, x_copies, o_copies = [], [], []
    for at, peer in enumerate(peers):
        q_copies.append(
            remote(
                qb.at[pl.ds(peer * share, share)],
                q_in.at[mine_rows],
                q_send.at[at],
                q_recv.at[at],
                "req",
                peer,
            )
        )
        q_copies[-1].start()
        o_copies.append(
            remote(
                o_ready.at[pl.ds(peer * share, share)],
                o_out.at[mine_rows],
                o_send.at[at],
                o_recv.at[at],
                "req",
                peer,
            )
        )
    for copy in q_copies:
        copy.wait_send()
    for portion in range(X_PARTS):
        cols = slice(portion * half, (portion + 1) * half)
        x_copies.append([])
        for at, peer in enumerate(peers):
            x_copies[-1].append(
                remote(
                    xb.at[peer, :, cols],
                    x_in.at[me, :, cols],
                    x_send.at[portion, at],
                    x_recv.at[portion, at],
                    "req",
                    peer,
                )
            )
            x_copies[-1][-1].start()

    def state_copy(tile):
        lanes = pl.ds(pl.multiple_of(tile * 128, 128), 128)
        return pltpu.make_async_copy(state.at[:, lanes], held.at[tile], state_sem.at[tile])

    for w_at in range(chunks):
        for split in range(splits):
            at = split * chunks + w_at
            cols = pl.ds(at * span, span)
            pltpu.make_async_copy(dt_proj.at[:, cols], rate_w.at[:, cols], chunk_sem.at[at]).start()
            for tile in range(tiles):
                state_copy(at * tiles + tile).start()
    part[...] = jnp.zeros_like(part)
    for copy in loads:
        copy.wait()
    own_q.wait()
    for copy in q_copies:
        copy.wait_recv()

    cache_len = list_len * pool.shape[2]
    scale = 1.0 / math.sqrt(HEAD_SIZE)
    recent = kv_heads * steps
    all_rows = kv_heads * q_rows
    group_width = q_rows // steps
    token = lax.broadcasted_iota(jnp.int32, (all_rows, cache_len), 1)
    column = lax.broadcasted_iota(jnp.int32, (all_rows, recent), 1)
    row = lax.broadcasted_iota(jnp.int32, (all_rows, recent), 0)
    row_head = row // q_rows
    row_moment = (row - row_head * q_rows) // group_width
    seen = (column >= row_head * steps) & (column <= row_head * steps + row_moment)
    contract = (((1,), (1,)), ((), ()))
    together = 4

    def some_requests(at, carry):
        reqs = [at * together + offset for offset in range(together)]
        rows = reqs
        reqs = [order[slot] for slot in rows]
        scores, fresh = [], []
        for req, slot in zip(reqs, rows):
            keys = jnp.concatenate([pool[table[req, i], 0] for i in range(list_len)], axis=0)
            parts = [
                lax.dot_general(
                    q_in[slot, head * q_rows : (head + 1) * q_rows, :],
                    keys[:, head * HEAD_SIZE : (head + 1) * HEAD_SIZE],
                    contract,
                    preferred_element_type=jnp.float32,
                )
                for head in range(kv_heads)
            ]
            scores.append(jnp.concatenate(parts, axis=0))
            fresh.append(
                lax.dot_general(
                    q_in[slot, :all_rows, :],
                    q_in[slot, all_rows : all_rows + recent, :],
                    contract,
                    preferred_element_type=jnp.float32,
                )
            )
        weights = []
        for req, old, new in zip(reqs, scores, fresh):
            old = jnp.where(token < lengths[req], old * scale, -jnp.inf)
            new = jnp.where(seen, new * scale, -jnp.inf)
            top = jnp.maximum(
                jnp.max(old, axis=1, keepdims=True), jnp.max(new, axis=1, keepdims=True)
            )
            old = jnp.exp(old - top)
            new = jnp.exp(new - top)
            total = jnp.sum(old, axis=1, keepdims=True) + jnp.sum(new, axis=1, keepdims=True)
            weights.append((old.astype(jnp.bfloat16), new.astype(jnp.bfloat16), 1.0 / total))
        for req, slot, (old, new, inverse) in zip(reqs, rows, weights):
            values = jnp.concatenate([pool[table[req, i], 1] for i in range(list_len)], axis=0)
            parts = [
                jnp.dot(
                    old[head * q_rows : (head + 1) * q_rows, :],
                    values[:, head * HEAD_SIZE : (head + 1) * HEAD_SIZE],
                    preferred_element_type=jnp.float32,
                )
                for head in range(kv_heads)
            ]
            mixed = jnp.concatenate(parts, axis=0) + jnp.dot(
                new,
                q_in[slot, all_rows + recent : all_rows + 2 * recent, :],
                preferred_element_type=jnp.float32,
            )
            o_ready[slot] = (mixed * inverse).astype(jnp.bfloat16)
        return carry

    lax.fori_loop(0, local_reqs // together, some_requests, 0)

    own_x.wait()
    for portion in range(X_PARTS):
        for copy in x_copies[portion]:
            copy.wait_recv()
        for split in range(splits):

            def conv_chunk(at, carry):
                inner = pl.ds(pl.multiple_of(at * chunk, chunk), chunk)
                outer = pl.ds(pl.multiple_of(split * block_width + at * chunk, chunk), chunk)
                block = x_in[:, :, inner].reshape(n * BLOCK_ROWS, chunk)
                fresh = jnp.dot(place[split], block, preferred_element_type=jnp.float32)
                window = [conv_rows[row, :, outer].astype(jnp.float32) for row in range(taps - 1)]
                window += [fresh[t * local_reqs : (t + 1) * local_reqs] for t in range(steps)]
                for t in range(steps):
                    total = conv_bias[:, outer] + sum(
                        conv_weight[tap : tap + 1, outer] * window[t + tap] for tap in range(taps)
                    )
                    active = total / (1.0 + jnp.exp(-total))
                    conv_out[t * local_reqs : (t + 1) * local_reqs, outer] = active.astype(jnp.bfloat16)
                part[:, :proj_width] += lax.dot_general(
                    conv_out[:, outer],
                    proj_w[:, outer],
                    (((1,), (1,)), ((), ())),
                    preferred_element_type=jnp.float32,
                )
                return carry

            lax.fori_loop(
                portion * (half // chunk), (portion + 1) * (half // chunk), conv_chunk, 0
            )
        if portion == 0:
            for copies in x_copies:
                for copy in copies:
                    copy.wait_send()
            for copy in o_copies:
                copy.start()
            own_o = pltpu.make_async_copy(
                o_ready.at[mine_rows], o_out.at[mine_rows], local_sem.at[2]
            )
            own_o.start()
    copies = []
    for step in range(1, width):
        peer = lax.rem(lane + step, width)
        copies.append(
            remote(
                part.at[pl.ds(pl.multiple_of(peer * piece, piece), piece)],
                gathered.at[step],
                rs_send.at[step],
                rs_recv.at[step],
                "tp",
                peer,
            )
        )
        copies[-1].start()
    mine = pl.ds(pl.multiple_of(lane * piece, piece), piece)
    gathered[0] = part[mine, :]
    for copy in copies:
        copy.wait()
    summed = gathered[0]
    for step in range(1, width):
        summed = summed + gathered[step]
    dt_low = summed[:, :rank_width]
    scale = lax.rsqrt(jnp.mean(dt_low * dt_low, axis=-1, keepdims=True) + EPSILON)
    normed[mine, :] = (dt_low * scale * dt_gain[...]).astype(jnp.bfloat16)
    coefs[mine, :] = summed[:, rank_width:]
    copies = []
    for step in range(1, width):
        peer = lax.rem(lane + step, width)
        for at, ref in enumerate((normed, coefs)):
            copies.append(
                remote(
                    ref.at[mine], ref.at[mine], ag_send.at[at, step], ag_recv.at[at, step], "tp", peer
                )
            )
            copies[-1].start()
    for copy in copies:
        copy.wait()
    for t in range(steps):
        at_rows = slice(t * local_reqs, (t + 1) * local_reqs)
        for entry in range(state_size):
            for wide, column in ((b_wide, entry), (c_wide, state_size + entry)):
                wide[t, entry] = jnp.broadcast_to(
                    coefs[at_rows, column : column + 1], (local_reqs, 128)
                )
    groups = local_reqs // 8

    def scan_chunk(w_at, carry):
        inner = pl.ds(pl.multiple_of(w_at * span, span), span)
        blocks = jnp.zeros((n * BLOCK_ROWS, span), jnp.float32)
        for split in range(splits):
            at = split * spans + w_at
            outer = pl.ds(pl.multiple_of(at * span, span), span)
            pltpu.make_async_copy(
                dt_proj.at[:, outer], rate_w.at[:, outer], chunk_sem.at[at]
            ).wait()
            raw = (
                jnp.dot(normed[...], rate_w[:, outer], preferred_element_type=jnp.float32)
                + dt_bias[:, outer]
            )
            rate = jnp.maximum(raw, 0.0) + jnp.log1p(jnp.exp(-jnp.abs(raw)))
            inputs = conv_out[:, outer].astype(jnp.float32)
            rates[...] = rate
            drives[...] = rate * inputs
            decay[...] = jnp.exp(a_log[:, outer]) * (-LOG2E)
            for tile in range(tiles):
                state_copy(at * tiles + tile).wait()

            def one_tile(cell, inner_carry):
                tile = cell // groups
                first = pl.multiple_of((cell - tile * groups) * 8, 8)
                lanes = pl.ds(pl.multiple_of(tile * 128, 128), 128)
                rows_at = [pl.ds(pl.multiple_of(t * local_reqs + first, 8), 8) for t in range(steps)]
                rate_t = [rates[rows_at[t], lanes] for t in range(steps)]
                drive_t = [drives[rows_at[t], lanes] for t in range(steps)]
                sums = [jnp.zeros((8, 128), jnp.float32) for _ in range(steps)]
                for entry in range(state_size):
                    hidden = held[
                        at * tiles + tile, pl.ds(first * state_size + entry, 8, stride=state_size), :
                    ]
                    slope = decay[entry : entry + 1, lanes]
                    for t in range(steps):
                        hidden = (
                            jnp.exp2(rate_t[t] * slope) * hidden
                            + drive_t[t] * b_wide[t, entry, pl.ds(first, 8), :]
                        )
                        sums[t] = sums[t] + hidden * c_wide[t, entry, pl.ds(first, 8), :]
                for t in range(steps):
                    readings[rows_at[t], lanes] = sums[t]
                return inner_carry

            lax.fori_loop(0, tiles * groups, one_tile, 0)
            reading = (readings[...] + skip_d[:, outer] * inputs).astype(jnp.bfloat16)
            blocks = blocks + jnp.dot(
                place_back[split], reading, preferred_element_type=jnp.float32
            )
        ready[:, :, inner] = blocks.astype(jnp.bfloat16).reshape(n, BLOCK_ROWS, span)
        for step in range(1, n):
            peer = lax.rem(me + step, n)
            remote(
                ready.at[peer, :, inner],
                y_out.at[me, :, inner],
                y_send.at[step],
                y_recv.at[step],
                "req",
                peer,
            ).start()
        return carry

    lax.fori_loop(0, chunks, scan_chunk, 0)
    own_y = pltpu.make_async_copy(ready.at[me], y_out.at[me], local_sem.at[3])
    own_y.start()
    own_o.wait()
    for copy in o_copies:
        copy.wait()
    for step in range(1, n):
        peer = lax.rem(me + step, n)
        remote(
            ready.at[peer], y_out.at[me], y_send.at[step], y_recv.at[step], "req", peer
        ).wait()
    own_y.wait()


def scan_chunk_of(block_width):
    return min(512, block_width)


def decode(
    table,
    lengths,
    order,
    qb,
    xb,
    pool,
    conv_rows,
    place,
    place_back,
    conv_weight,
    conv_bias,
    x_proj,
    dt_gain,
    dt_proj,
    dt_bias,
    a_log,
    skip_d,
    state,
    kv_heads,
    q_rows,
    steps,
):
    n = xb.shape[0]
    width = lax.axis_size("tp")
    local_reqs = table.shape[0]
    rows = place.shape[1]
    state_size, channels = a_log.shape
    rank_width = dt_gain.shape[1]
    wide = rank_width + 128
    span = scan_chunk_of(xb.shape[2])
    dma = pltpu.SemaphoreType.DMA
    smem = pl.BlockSpec(memory_space=pltpu.SMEM)
    outs = jax.ShapeDtypeStruct((local_reqs, kv_heads * q_rows, HEAD_SIZE), jnp.bfloat16)
    return pl.pallas_call(
        functools.partial(decode_kernel, kv_heads, q_rows, steps),
        out_shape=(outs, jax.ShapeDtypeStruct(xb.shape, jnp.bfloat16)),
        in_specs=[smem] * 3 + [ANY] * 15,
        out_specs=(ANY, ANY),
        scratch_shapes=[
            like(pool),
            like(conv_rows),
            like(place),
            like(place_back),
            like(conv_weight),
            like(conv_bias),
            like(dt_gain),
            like(dt_bias),
            like(a_log),
            like(skip_d),
            like(x_proj),
            dma((11,)),
            like(qb),
            like(xb),
            like(outs),
            pltpu.VMEM((rows, channels), jnp.bfloat16),
            pltpu.VMEM((rows, wide), jnp.float32),
            pltpu.VMEM((width, rows // width, wide), jnp.float32),
            pltpu.VMEM((rows, rank_width), jnp.bfloat16),
            pltpu.VMEM((rows, 128), jnp.float32),
            pltpu.VMEM((steps, state_size, local_reqs, 128), jnp.float32),
            pltpu.VMEM((steps, state_size, local_reqs, 128), jnp.float32),
            pltpu.VMEM((state_size, span), jnp.float32),
            pltpu.VMEM((channels // 128, local_reqs * state_size, 128), jnp.float32),
            like(dt_proj),
            pltpu.VMEM((rows, span), jnp.float32),
            pltpu.VMEM((rows, span), jnp.float32),
            pltpu.VMEM((rows, span), jnp.float32),
            like(xb),
            dma((n,)),
            dma((n,)),
            dma((X_PARTS, n)),
            dma((X_PARTS, n)),
            dma((n,)),
            dma((n,)),
            dma((n,)),
            dma((n,)),
            dma((4,)),
            dma((channels // span,)),
            dma((channels // 128,)),
            dma((width,)),
            dma((width,)),
            dma((2, width)),
            dma((2, width)),
        ],
        compiler_params=pltpu.CompilerParams(
            collective_id=0, has_side_effects=True, vmem_limit_bytes=VMEM_LIMIT
        ),
    )(
        table,
        lengths,
        order,
        qb,
        xb,
        pool,
        conv_rows,
        place,
        place_back,
        conv_weight,
        conv_bias,
        x_proj,
        dt_gain,
        dt_proj,
        dt_bias,
        a_log,
        skip_d,
        state,
    )


def per_device(
    queries,
    new_kv,
    prefill_page_pool,
    page_table,
    prompt_len,
    dest_device,
    ssm_state,
    conv_state,
    mamba_x,
    mamba_z,
    conv_weight,
    conv_bias,
    x_proj,
    dt_gain,
    dt_proj,
    dt_bias,
    a_log,
    skip_d,
):
    n = lax.axis_size("req")
    local_reqs = dest_device.shape[0]
    steps = queries.shape[0]
    channels = mamba_x.shape[2]
    kv_heads = prefill_page_pool.shape[3] // HEAD_SIZE
    group_width = queries.shape[2] // HEAD_SIZE // kv_heads
    q_rows = steps * group_width
    state_size = a_log.shape[0]
    share = local_reqs // n
    splits = BLOCK_ROWS // (steps * share)
    block_width = channels // splits
    index = jnp.arange(local_reqs, dtype=jnp.int32)
    same = dest_device[:, None] == dest_device[None, :]
    rank = jnp.sum((same & (index[None, :] < index[:, None])).astype(jnp.int32), axis=1)
    slots = dest_device * share + rank
    order = jnp.sum(jnp.where(slots[:, None] == index[None, :], index[:, None], 0), axis=0)
    times = jnp.arange(steps, dtype=jnp.int32)
    split_ids = jnp.arange(splits, dtype=jnp.int32)
    block_row = dest_device * BLOCK_ROWS + rank * splits
    block_row = (
        block_row[None, None, :]
        + times[None, :, None] * (share * splits)
        + split_ids[:, None, None]
    ).reshape(splits, steps * local_reqs)
    block_ids = jnp.arange(n * BLOCK_ROWS, dtype=jnp.int32)
    place = (block_row[:, :, None] == block_ids[None, None, :]).astype(jnp.bfloat16)
    place_back = (block_row[:, None, :] == block_ids[None, :, None]).astype(jnp.bfloat16)

    xb = jnp.transpose(
        mamba_x.reshape(steps, n, share, channels), (1, 0, 2, 3)
    ).reshape(n, BLOCK_ROWS, block_width)
    q_part = jnp.transpose(
        queries.reshape(steps, local_reqs, kv_heads, group_width, HEAD_SIZE), (1, 2, 0, 3, 4)
    ).reshape(local_reqs, kv_heads * q_rows, HEAD_SIZE)
    kv_part = jnp.transpose(
        new_kv.reshape(steps, local_reqs, 2, kv_heads, HEAD_SIZE), (1, 2, 3, 0, 4)
    ).reshape(local_reqs, 2 * kv_heads * steps, HEAD_SIZE)
    slabs = jnp.concatenate([q_part, kv_part], axis=1)
    o_back, y_back = decode(
        page_table,
        prompt_len,
        order,
        slabs,
        xb,
        prefill_page_pool,
        jnp.transpose(conv_state, (1, 0, 2)),
        place,
        place_back,
        conv_weight,
        conv_bias[None],
        x_proj.T,
        dt_gain[None],
        dt_proj,
        dt_bias[None],
        a_log,
        skip_d[None],
        ssm_state.reshape(local_reqs * state_size, channels),
        kv_heads,
        q_rows,
        steps,
    )
    attn_out = jnp.transpose(
        o_back.reshape(local_reqs, kv_heads, steps, group_width, HEAD_SIZE), (2, 0, 1, 3, 4)
    ).reshape(queries.shape)
    reading = jnp.transpose(
        y_back.reshape(n, steps, share, channels), (1, 0, 2, 3)
    ).reshape(mamba_x.shape)
    gate_values = jax.nn.silu(mamba_z.astype(jnp.float32))
    mamba_out = (reading.astype(jnp.float32) * gate_values).astype(jnp.bfloat16)
    return (attn_out, mamba_out)


def solution(mesh):
    return jax.shard_map(
        per_device,
        mesh=mesh,
        in_specs=(
            P(None, "req", "tp"),
            P(None, "req", None, "tp"),
            P("req", None, None, "tp"),
            P("req", None),
            P("req"),
            P("req"),
            P("req", None, "tp"),
            P("req", None, "tp"),
            P(None, "req", "tp"),
            P(None, "req", "tp"),
            P(None, "tp"),
            P("tp"),
            P("tp", None),
            P(),
            P(None, "tp"),
            P("tp"),
            P(None, "tp"),
            P("tp"),
        ),
        out_specs=(P(None, "req", "tp"), P(None, "req", "tp")),
        check_vma=False,
    )
```

```python
import functools
import math

import jax
import jax.numpy as jnp
from jax import lax
from jax.experimental import pallas as pl
from jax.experimental.pallas import tpu as pltpu
from jax.sharding import PartitionSpec as P

HEAD_SIZE = 128
BLOCK_ROWS = 16
X_PARTS = 2
TILES_TOGETHER = 2
EPSILON = 1e-06
LOG2E = 1.4426950408889634
VMEM_LIMIT = 56 * 1024 * 1024
MESH = pl.DeviceIdType.MESH
ANY = pl.BlockSpec(memory_space=pl.ANY)
VMEM = pl.BlockSpec(memory_space=pltpu.VMEM)


def greet(axes):
    barrier = pltpu.get_barrier_semaphore()
    total = 0
    for name in axes:
        size = lax.axis_size(name)
        me = lax.axis_index(name)
        for step in range(1, size):
            pl.semaphore_signal(
                barrier, inc=1, device_id={name: lax.rem(me + step, size)}, device_id_type=MESH
            )
        total += size - 1
    pl.semaphore_wait(barrier, total)


def remote(src, dst, send_sem, recv_sem, axis, peer):
    return pltpu.make_async_remote_copy(
        src_ref=src,
        dst_ref=dst,
        send_sem=send_sem,
        recv_sem=recv_sem,
        device_id={axis: peer},
        device_id_type=MESH,
    )


def bring(sems, *pairs):
    copies = [
        pltpu.make_async_copy(src, dst, sems.at[at]) for at, (src, dst) in enumerate(pairs)
    ]
    for copy in copies:
        copy.start()
    return copies


def like(value):
    return pltpu.VMEM(value.shape, value.dtype)


def decode_kernel(
    kv_heads,
    q_rows,
    steps,
    table,
    lengths,
    order,
    qb,
    xb,
    pool_far,
    conv_rows_far,
    place_far,
    place_back_far,
    conv_weight_far,
    conv_bias_far,
    x_proj,
    dt_gain_far,
    dt_proj,
    dt_bias_far,
    a_log_far,
    skip_d_far,
    state,
    o_out,
    y_out,
    pool,
    conv_rows,
    place,
    place_back,
    conv_weight,
    conv_bias,
    dt_gain,
    dt_bias,
    a_log,
    skip_d,
    proj_w,
    load_sem,
    q_in,
    x_in,
    o_ready,
    conv_out,
    part,
    gathered,
    normed,
    coefs,
    b_wide,
    c_wide,
    decay,
    held,
    rate_w,
    rates,
    drives,
    readings,
    ready,
    q_send,
    q_recv,
    x_send,
    x_recv,
    o_send,
    o_recv,
    y_send,
    y_recv,
    local_sem,
    chunk_sem,
    state_sem,
    rs_send,
    rs_recv,
    ag_send,
    ag_recv,
):
    n = lax.axis_size("req")
    width = lax.axis_size("tp")
    me = lax.axis_index("req")
    lane = lax.axis_index("tp")
    splits, rows, _ = place.shape
    block_width = xb.shape[2]
    list_len, local_reqs = table.shape
    share = local_reqs // n
    state_size, channels = a_log.shape
    taps = conv_weight.shape[0]
    rank_width = dt_gain.shape[1]
    proj_width = x_proj.shape[0]
    piece = rows // width
    half = block_width // X_PARTS
    chunk = min(512, half)
    span = scan_chunk_of(block_width)
    chunks = block_width // span
    spans = chunks
    tiles = span // 128
    mine_rows = pl.ds(me * share, share)
    own_q = pltpu.make_async_copy(qb.at[mine_rows], q_in.at[mine_rows], local_sem.at[0])
    own_q.start()
    own_x = pltpu.make_async_copy(xb.at[me], x_in.at[me], local_sem.at[1])
    own_x.start()
    loads = bring(
        load_sem,
        (pool_far, pool),
        (x_proj, proj_w),
        (conv_rows_far, conv_rows),
        (place_far, place),
        (place_back_far, place_back),
        (conv_weight_far, conv_weight),
        (conv_bias_far, conv_bias),
        (dt_gain_far, dt_gain),
        (dt_bias_far, dt_bias),
        (a_log_far, a_log),
        (skip_d_far, skip_d),
    )
    greet(("req", "tp"))
    peers = [lax.rem(me + step, n) for step in range(1, n)]
    q_copies, x_copies, o_copies = [], [], []
    for at, peer in enumerate(peers):
        q_copies.append(
            remote(
                qb.at[pl.ds(peer * share, share)],
                q_in.at[mine_rows],
                q_send.at[at],
                q_recv.at[at],
                "req",
                peer,
            )
        )
        q_copies[-1].start()
        o_copies.append(
            remote(
                o_ready.at[pl.ds(peer * share, share)],
                o_out.at[mine_rows],
                o_send.at[at],
                o_recv.at[at],
                "req",
                peer,
            )
        )
    for copy in q_copies:
        copy.wait_send()
    for portion in range(X_PARTS):
        cols = slice(portion * half, (portion + 1) * half)
        x_copies.append([])
        for at, peer in enumerate(peers):
            x_copies[-1].append(
                remote(
                    xb.at[peer, :, cols],
                    x_in.at[me, :, cols],
                    x_send.at[portion, at],
                    x_recv.at[portion, at],
                    "req",
                    peer,
                )
            )
            x_copies[-1][-1].start()

    def state_copy(tile):
        lanes = pl.ds(pl.multiple_of(tile * 128, 128), 128)
        return pltpu.make_async_copy(state.at[:, lanes], held.at[tile], state_sem.at[tile])

    for w_at in range(chunks):
        for split in range(splits):
            at = split * chunks + w_at
            cols = pl.ds(at * span, span)
            pltpu.make_async_copy(dt_proj.at[:, cols], rate_w.at[:, cols], chunk_sem.at[at]).start()
            for tile in range(tiles):
                state_copy(at * tiles + tile).start()
    part[...] = jnp.zeros_like(part)
    for copy in loads:
        copy.wait()
    own_q.wait()
    for copy in q_copies:
        copy.wait_recv()

    cache_len = list_len * pool.shape[2]
    scale = 1.0 / math.sqrt(HEAD_SIZE)
    recent = kv_heads * steps
    all_rows = kv_heads * q_rows
    group_width = q_rows // steps
    token = lax.broadcasted_iota(jnp.int32, (all_rows, cache_len), 1)
    column = lax.broadcasted_iota(jnp.int32, (all_rows, recent), 1)
    row = lax.broadcasted_iota(jnp.int32, (all_rows, recent), 0)
    row_head = row // q_rows
    row_moment = (row - row_head * q_rows) // group_width
    seen = (column >= row_head * steps) & (column <= row_head * steps + row_moment)
    contract = (((1,), (1,)), ((), ()))
    together = 4

    def some_requests(at, carry):
        reqs = [at * together + offset for offset in range(together)]
        rows = reqs
        reqs = [order[slot] for slot in rows]
        scores, fresh = [], []
        for req, slot in zip(reqs, rows):
            keys = jnp.concatenate([pool[table[i, req], 0] for i in range(list_len)], axis=0)
            parts = [
                lax.dot_general(
                    q_in[slot, head * q_rows : (head + 1) * q_rows, :],
                    keys[:, head * HEAD_SIZE : (head + 1) * HEAD_SIZE],
                    contract,
                    preferred_element_type=jnp.float32,
                )
                for head in range(kv_heads)
            ]
            scores.append(jnp.concatenate(parts, axis=0))
            fresh.append(
                lax.dot_general(
                    q_in[slot, :all_rows, :],
                    q_in[slot, all_rows : all_rows + recent, :],
                    contract,
                    preferred_element_type=jnp.float32,
                )
            )
        weights = []
        for req, old, new in zip(reqs, scores, fresh):
            old = jnp.where(token < lengths[req], old * scale, -jnp.inf)
            new = jnp.where(seen, new * scale, -jnp.inf)
            top = jnp.maximum(
                jnp.max(old, axis=1, keepdims=True), jnp.max(new, axis=1, keepdims=True)
            )
            old = jnp.exp(old - top)
            new = jnp.exp(new - top)
            total = jnp.sum(old, axis=1, keepdims=True) + jnp.sum(new, axis=1, keepdims=True)
            weights.append((old.astype(jnp.bfloat16), new.astype(jnp.bfloat16), 1.0 / total))
        for req, slot, (old, new, inverse) in zip(reqs, rows, weights):
            values = jnp.concatenate([pool[table[i, req], 1] for i in range(list_len)], axis=0)
            parts = [
                jnp.dot(
                    old[head * q_rows : (head + 1) * q_rows, :],
                    values[:, head * HEAD_SIZE : (head + 1) * HEAD_SIZE],
                    preferred_element_type=jnp.float32,
                )
                for head in range(kv_heads)
            ]
            mixed = jnp.concatenate(parts, axis=0) + jnp.dot(
                new,
                q_in[slot, all_rows + recent : all_rows + 2 * recent, :],
                preferred_element_type=jnp.float32,
            )
            o_ready[slot] = (mixed * inverse).astype(jnp.bfloat16)
        return carry

    lax.fori_loop(0, local_reqs // together, some_requests, 0)

    own_x.wait()
    for portion in range(X_PARTS):
        for copy in x_copies[portion]:
            copy.wait_recv()
        for split in range(splits):

            def conv_chunk(at, carry):
                inner = pl.ds(pl.multiple_of(at * chunk, chunk), chunk)
                outer = pl.ds(pl.multiple_of(split * block_width + at * chunk, chunk), chunk)
                block = x_in[:, :, inner].reshape(n * BLOCK_ROWS, chunk)
                fresh = jnp.dot(place[split], block, preferred_element_type=jnp.float32)
                window = [conv_rows[row, :, outer].astype(jnp.float32) for row in range(taps - 1)]
                window += [fresh[t * local_reqs : (t + 1) * local_reqs] for t in range(steps)]
                for t in range(steps):
                    total = conv_bias[:, outer] + sum(
                        conv_weight[tap : tap + 1, outer] * window[t + tap] for tap in range(taps)
                    )
                    active = total / (1.0 + jnp.exp(-total))
                    conv_out[t * local_reqs : (t + 1) * local_reqs, outer] = active.astype(jnp.bfloat16)
                part[:, :proj_width] += lax.dot_general(
                    conv_out[:, outer],
                    proj_w[:, outer],
                    (((1,), (1,)), ((), ())),
                    preferred_element_type=jnp.float32,
                )
                return carry

            lax.fori_loop(
                portion * (half // chunk), (portion + 1) * (half // chunk), conv_chunk, 0
            )
        if portion == 0:
            for copies in x_copies:
                for copy in copies:
                    copy.wait_send()
            for copy in o_copies:
                copy.start()
            own_o = pltpu.make_async_copy(
                o_ready.at[mine_rows], o_out.at[mine_rows], local_sem.at[2]
            )
            own_o.start()
    copies = []
    for step in range(1, width):
        peer = lax.rem(lane + step, width)
        copies.append(
            remote(
                part.at[pl.ds(pl.multiple_of(peer * piece, piece), piece)],
                gathered.at[step],
                rs_send.at[step],
                rs_recv.at[step],
                "tp",
                peer,
            )
        )
        copies[-1].start()
    mine = pl.ds(pl.multiple_of(lane * piece, piece), piece)
    gathered[0] = part[mine, :]
    for copy in copies:
        copy.wait()
    summed = gathered[0]
    for step in range(1, width):
        summed = summed + gathered[step]
    dt_low = summed[:, :rank_width]
    scale = lax.rsqrt(jnp.mean(dt_low * dt_low, axis=-1, keepdims=True) + EPSILON)
    normed[mine, :] = (dt_low * scale * dt_gain[...]).astype(jnp.bfloat16)
    coefs[mine, :] = summed[:, rank_width:]
    copies = []
    for step in range(1, width):
        peer = lax.rem(lane + step, width)
        for at, ref in enumerate((normed, coefs)):
            copies.append(
                remote(
                    ref.at[mine], ref.at[mine], ag_send.at[at, step], ag_recv.at[at, step], "tp", peer
                )
            )
            copies[-1].start()
    for copy in copies:
        copy.wait()
    for t in range(steps):
        at_rows = slice(t * local_reqs, (t + 1) * local_reqs)
        for entry in range(state_size):
            for wide, column in ((b_wide, entry), (c_wide, state_size + entry)):
                wide[t, entry] = jnp.broadcast_to(
                    coefs[at_rows, column : column + 1], (local_reqs, 128)
                )
    groups = local_reqs // 8

    def scan_chunk(w_at, carry):
        inner = pl.ds(pl.multiple_of(w_at * span, span), span)
        blocks = jnp.zeros((n * BLOCK_ROWS, span), jnp.float32)
        for split in range(splits):
            at = split * spans + w_at
            outer = pl.ds(pl.multiple_of(at * span, span), span)
            pltpu.make_async_copy(
                dt_proj.at[:, outer], rate_w.at[:, outer], chunk_sem.at[at]
            ).wait()
            raw = (
                jnp.dot(normed[...], rate_w[:, outer], preferred_element_type=jnp.float32)
                + dt_bias[:, outer]
            )
            rate = jnp.maximum(raw, 0.0) + jnp.log1p(jnp.exp(-jnp.abs(raw)))
            inputs = conv_out[:, outer].astype(jnp.float32)
            rates[...] = rate
            drives[...] = rate * inputs
            decay[...] = jnp.exp(a_log[:, outer]) * (-LOG2E)
            for tile in range(tiles):
                state_copy(at * tiles + tile).wait()

            def one_cell(cell, inner_carry):
                pair = cell // groups
                first = pl.multiple_of((cell - pair * groups) * 8, 8)
                subs = range(TILES_TOGETHER)
                lanes = [
                    pl.ds(pl.multiple_of((pair * TILES_TOGETHER + sub) * 128, 128), 128)
                    for sub in subs
                ]
                rows_at = [pl.ds(pl.multiple_of(t * local_reqs + first, 8), 8) for t in range(steps)]
                rate_t = [[rates[rows_at[t], lanes[sub]] for sub in subs] for t in range(steps)]
                drive_t = [[drives[rows_at[t], lanes[sub]] for sub in subs] for t in range(steps)]
                sums = [[jnp.zeros((8, 128), jnp.float32) for _ in subs] for _ in range(steps)]
                for entry in range(state_size):
                    entry_rows = pl.ds(first * state_size + entry, 8, stride=state_size)
                    hidden = [
                        held[at * tiles + pair * TILES_TOGETHER + sub, entry_rows, :] for sub in subs
                    ]
                    slope = [decay[entry : entry + 1, lanes[sub]] for sub in subs]
                    for t in range(steps):
                        b_now = b_wide[t, entry, pl.ds(first, 8), :]
                        c_now = c_wide[t, entry, pl.ds(first, 8), :]
                        for sub in subs:
                            hidden[sub] = (
                                jnp.exp2(rate_t[t][sub] * slope[sub]) * hidden[sub]
                                + drive_t[t][sub] * b_now
                            )
                            sums[t][sub] = sums[t][sub] + hidden[sub] * c_now
                for t in range(steps):
                    for sub in subs:
                        readings[rows_at[t], lanes[sub]] = sums[t][sub]
                return inner_carry

            lax.fori_loop(0, tiles // TILES_TOGETHER * groups, one_cell, 0)
            reading = (readings[...] + skip_d[:, outer] * inputs).astype(jnp.bfloat16)
            blocks = blocks + jnp.dot(
                place_back[split], reading, preferred_element_type=jnp.float32
            )
        ready[:, :, inner] = blocks.astype(jnp.bfloat16).reshape(n, BLOCK_ROWS, span)
        for step in range(1, n):
            peer = lax.rem(me + step, n)
            remote(
                ready.at[peer, :, inner],
                y_out.at[me, :, inner],
                y_send.at[step],
                y_recv.at[step],
                "req",
                peer,
            ).start()
        return carry

    lax.fori_loop(0, chunks, scan_chunk, 0)
    own_y = pltpu.make_async_copy(ready.at[me], y_out.at[me], local_sem.at[3])
    own_y.start()
    own_o.wait()
    for copy in o_copies:
        copy.wait()
    for step in range(1, n):
        peer = lax.rem(me + step, n)
        remote(
            ready.at[peer], y_out.at[me], y_send.at[step], y_recv.at[step], "req", peer
        ).wait()
    own_y.wait()


def scan_chunk_of(block_width):
    return min(512, block_width)


def decode(
    table,
    lengths,
    order,
    qb,
    xb,
    pool,
    conv_rows,
    place,
    place_back,
    conv_weight,
    conv_bias,
    x_proj,
    dt_gain,
    dt_proj,
    dt_bias,
    a_log,
    skip_d,
    state,
    kv_heads,
    q_rows,
    steps,
):
    n = xb.shape[0]
    width = lax.axis_size("tp")
    local_reqs = table.shape[1]
    rows = place.shape[1]
    state_size, channels = a_log.shape
    rank_width = dt_gain.shape[1]
    wide = rank_width + 128
    span = scan_chunk_of(xb.shape[2])
    dma = pltpu.SemaphoreType.DMA
    smem = pl.BlockSpec(memory_space=pltpu.SMEM)
    outs = jax.ShapeDtypeStruct((local_reqs, kv_heads * q_rows, HEAD_SIZE), jnp.bfloat16)
    return pl.pallas_call(
        functools.partial(decode_kernel, kv_heads, q_rows, steps),
        out_shape=(outs, jax.ShapeDtypeStruct(xb.shape, jnp.bfloat16)),
        in_specs=[smem] * 3 + [ANY] * 15,
        out_specs=(ANY, ANY),
        scratch_shapes=[
            like(pool),
            like(conv_rows),
            like(place),
            like(place_back),
            like(conv_weight),
            like(conv_bias),
            like(dt_gain),
            like(dt_bias),
            like(a_log),
            like(skip_d),
            like(x_proj),
            dma((11,)),
            like(qb),
            like(xb),
            like(outs),
            pltpu.VMEM((rows, channels), jnp.bfloat16),
            pltpu.VMEM((rows, wide), jnp.float32),
            pltpu.VMEM((width, rows // width, wide), jnp.float32),
            pltpu.VMEM((rows, rank_width), jnp.bfloat16),
            pltpu.VMEM((rows, 128), jnp.float32),
            pltpu.VMEM((steps, state_size, local_reqs, 128), jnp.float32),
            pltpu.VMEM((steps, state_size, local_reqs, 128), jnp.float32),
            pltpu.VMEM((state_size, span), jnp.float32),
            pltpu.VMEM((channels // 128, local_reqs * state_size, 128), jnp.float32),
            like(dt_proj),
            pltpu.VMEM((rows, span), jnp.float32),
            pltpu.VMEM((rows, span), jnp.float32),
            pltpu.VMEM((rows, span), jnp.float32),
            like(xb),
            dma((n,)),
            dma((n,)),
            dma((X_PARTS, n)),
            dma((X_PARTS, n)),
            dma((n,)),
            dma((n,)),
            dma((n,)),
            dma((n,)),
            dma((4,)),
            dma((channels // span,)),
            dma((channels // 128,)),
            dma((width,)),
            dma((width,)),
            dma((2, width)),
            dma((2, width)),
        ],
        compiler_params=pltpu.CompilerParams(
            collective_id=0, has_side_effects=True, vmem_limit_bytes=VMEM_LIMIT
        ),
    )(
        table,
        lengths,
        order,
        qb,
        xb,
        pool,
        conv_rows,
        place,
        place_back,
        conv_weight,
        conv_bias,
        x_proj,
        dt_gain,
        dt_proj,
        dt_bias,
        a_log,
        skip_d,
        state,
    )


def per_device(
    queries,
    new_kv,
    prefill_page_pool,
    page_table,
    prompt_len,
    dest_device,
    ssm_state,
    conv_state,
    mamba_x,
    mamba_z,
    conv_weight,
    conv_bias,
    x_proj,
    dt_gain,
    dt_proj,
    dt_bias,
    a_log,
    skip_d,
):
    n = lax.axis_size("req")
    local_reqs = dest_device.shape[0]
    steps = queries.shape[0]
    channels = mamba_x.shape[2]
    kv_heads = prefill_page_pool.shape[3] // HEAD_SIZE
    group_width = queries.shape[2] // HEAD_SIZE // kv_heads
    q_rows = steps * group_width
    state_size = a_log.shape[0]
    share = local_reqs // n
    splits = BLOCK_ROWS // (steps * share)
    block_width = channels // splits
    index = jnp.arange(local_reqs, dtype=jnp.int32)
    same = dest_device[:, None] == dest_device[None, :]
    rank = jnp.sum((same & (index[None, :] < index[:, None])).astype(jnp.int32), axis=1)
    slots = dest_device * share + rank
    order = jnp.sum(jnp.where(slots[:, None] == index[None, :], index[:, None], 0), axis=0)
    times = jnp.arange(steps, dtype=jnp.int32)
    split_ids = jnp.arange(splits, dtype=jnp.int32)
    block_row = dest_device * BLOCK_ROWS + rank * splits
    block_row = (
        block_row[None, None, :]
        + times[None, :, None] * (share * splits)
        + split_ids[:, None, None]
    ).reshape(splits, steps * local_reqs)
    block_ids = jnp.arange(n * BLOCK_ROWS, dtype=jnp.int32)
    place = (block_row[:, :, None] == block_ids[None, None, :]).astype(jnp.bfloat16)
    place_back = (block_row[:, None, :] == block_ids[None, :, None]).astype(jnp.bfloat16)

    decode_row = (
        index[None, :] // share * BLOCK_ROWS
        + (times[:, None] * share + index[None, :] % share) * splits
    ).reshape(1, steps * local_reqs) + split_ids[:, None]
    home = (decode_row[:, :, None] == block_ids[None, None, :]).astype(jnp.bfloat16)
    flat_x = mamba_x.reshape(steps * local_reqs, channels)
    xb = sum(
        jnp.einsum("pb,pc->bc", home[at], flat_x[:, at * block_width : (at + 1) * block_width])
        for at in range(splits)
    ).reshape(n, BLOCK_ROWS, block_width)
    q_part = jnp.transpose(
        queries.reshape(steps, local_reqs, kv_heads, group_width, HEAD_SIZE), (1, 2, 0, 3, 4)
    ).reshape(local_reqs, kv_heads * q_rows, HEAD_SIZE)
    kv_part = jnp.transpose(
        new_kv.reshape(steps, local_reqs, 2, kv_heads, HEAD_SIZE), (1, 2, 3, 0, 4)
    ).reshape(local_reqs, 2 * kv_heads * steps, HEAD_SIZE)
    slabs = jnp.concatenate([q_part, kv_part], axis=1)
    o_back, y_back = decode(
        page_table.T,
        prompt_len,
        order,
        slabs,
        xb,
        prefill_page_pool,
        jnp.transpose(conv_state, (1, 0, 2)),
        place,
        place_back,
        conv_weight,
        conv_bias[None],
        x_proj.T,
        dt_gain[None],
        dt_proj,
        dt_bias[None],
        a_log,
        skip_d[None],
        ssm_state.reshape(local_reqs * state_size, channels),
        kv_heads,
        q_rows,
        steps,
    )
    attn_out = jnp.transpose(
        o_back.reshape(local_reqs, kv_heads, steps, group_width, HEAD_SIZE), (2, 0, 1, 3, 4)
    ).reshape(queries.shape)
    flat_y = y_back.reshape(n * BLOCK_ROWS, block_width)
    reading = jnp.concatenate(
        [
            jnp.einsum("pb,bc->pc", home[at], flat_y, preferred_element_type=jnp.float32)
            for at in range(splits)
        ],
        axis=1,
    )
    gate_values = jax.nn.silu(mamba_z.astype(jnp.float32)).reshape(reading.shape)
    mamba_out = (reading * gate_values).astype(jnp.bfloat16).reshape(mamba_x.shape)
    return (attn_out, mamba_out)


def solution(mesh):
    return jax.shard_map(
        per_device,
        mesh=mesh,
        in_specs=(
            P(None, "req", "tp"),
            P(None, "req", None, "tp"),
            P("req", None, None, "tp"),
            P("req", None),
            P("req"),
            P("req"),
            P("req", None, "tp"),
            P("req", None, "tp"),
            P(None, "req", "tp"),
            P(None, "req", "tp"),
            P(None, "tp"),
            P("tp"),
            P("tp", None),
            P(),
            P(None, "tp"),
            P("tp"),
            P(None, "tp"),
            P("tp"),
        ),
        out_specs=(P(None, "req", "tp"), P(None, "req", "tp")),
        check_vma=False,
    )
```

```python
import functools
import math

import jax
import jax.numpy as jnp
from jax import lax
from jax.experimental import pallas as pl
from jax.experimental.pallas import tpu as pltpu
from jax.sharding import PartitionSpec as P

HEAD_SIZE = 128
BLOCK_ROWS = 16
X_PARTS = 4
TILES_TOGETHER = 2
EPSILON = 1e-06
LOG2E = 1.4426950408889634
VMEM_LIMIT = 56 * 1024 * 1024
MESH = pl.DeviceIdType.MESH
ANY = pl.BlockSpec(memory_space=pl.ANY)
VMEM = pl.BlockSpec(memory_space=pltpu.VMEM)


def greet(axes):
    barrier = pltpu.get_barrier_semaphore()
    total = 0
    for name in axes:
        size = lax.axis_size(name)
        me = lax.axis_index(name)
        for step in range(1, size):
            pl.semaphore_signal(
                barrier, inc=1, device_id={name: lax.rem(me + step, size)}, device_id_type=MESH
            )
        total += size - 1
    pl.semaphore_wait(barrier, total)


def remote(src, dst, send_sem, recv_sem, axis, peer):
    return pltpu.make_async_remote_copy(
        src_ref=src,
        dst_ref=dst,
        send_sem=send_sem,
        recv_sem=recv_sem,
        device_id={axis: peer},
        device_id_type=MESH,
    )


def bring(sems, *pairs):
    copies = [
        pltpu.make_async_copy(src, dst, sems.at[at]) for at, (src, dst) in enumerate(pairs)
    ]
    for copy in copies:
        copy.start()
    return copies


def like(value):
    return pltpu.VMEM(value.shape, value.dtype)


def decode_kernel(
    kv_heads,
    q_rows,
    steps,
    table,
    lengths,
    order,
    qb,
    xb,
    pool_far,
    conv_rows_far,
    place_far,
    place_back_far,
    conv_weight_far,
    conv_bias_far,
    x_proj,
    dt_gain_far,
    dt_proj,
    dt_bias_far,
    a_log_far,
    skip_d_far,
    state,
    o_out,
    y_out,
    pool,
    conv_rows,
    place,
    place_back,
    conv_weight,
    conv_bias,
    dt_gain,
    dt_bias,
    a_log,
    skip_d,
    proj_w,
    load_sem,
    q_in,
    x_in,
    o_ready,
    conv_out,
    part,
    gathered,
    normed,
    coefs,
    b_wide,
    c_wide,
    decay,
    held,
    rate_w,
    rates,
    drives,
    readings,
    ready,
    q_send,
    q_recv,
    x_send,
    x_recv,
    o_send,
    o_recv,
    y_send,
    y_recv,
    local_sem,
    chunk_sem,
    state_sem,
    rs_send,
    rs_recv,
    ag_send,
    ag_recv,
):
    n = lax.axis_size("req")
    width = lax.axis_size("tp")
    me = lax.axis_index("req")
    lane = lax.axis_index("tp")
    splits, rows, _ = place.shape
    block_width = xb.shape[2]
    list_len, local_reqs = table.shape
    share = local_reqs // n
    state_size, channels = a_log.shape
    taps = conv_weight.shape[0]
    rank_width = dt_gain.shape[1]
    proj_width = x_proj.shape[0]
    piece = rows // width
    half = block_width // X_PARTS
    chunk = min(512, half)
    span = scan_chunk_of(block_width)
    chunks = block_width // span
    spans = chunks
    tiles = span // 128
    mine_rows = pl.ds(me * share, share)
    own_q = pltpu.make_async_copy(qb.at[mine_rows], q_in.at[mine_rows], local_sem.at[0])
    own_q.start()
    own_x = pltpu.make_async_copy(xb.at[me], x_in.at[me], local_sem.at[1])
    own_x.start()
    loads = bring(
        load_sem,
        (pool_far, pool),
        (x_proj, proj_w),
        (conv_rows_far, conv_rows),
        (place_far, place),
        (place_back_far, place_back),
        (conv_weight_far, conv_weight),
        (conv_bias_far, conv_bias),
        (dt_gain_far, dt_gain),
        (dt_bias_far, dt_bias),
        (a_log_far, a_log),
        (skip_d_far, skip_d),
    )
    greet(("req", "tp"))
    peers = [lax.rem(me + step, n) for step in range(1, n)]
    q_copies, x_copies, o_copies = [], [], []
    for at, peer in enumerate(peers):
        q_copies.append(
            remote(
                qb.at[pl.ds(peer * share, share)],
                q_in.at[mine_rows],
                q_send.at[at],
                q_recv.at[at],
                "req",
                peer,
            )
        )
        q_copies[-1].start()
        o_copies.append(
            remote(
                o_ready.at[pl.ds(peer * share, share)],
                o_out.at[mine_rows],
                o_send.at[at],
                o_recv.at[at],
                "req",
                peer,
            )
        )
    for copy in q_copies:
        copy.wait_send()
    for portion in range(X_PARTS):
        cols = slice(portion * half, (portion + 1) * half)
        x_copies.append([])
        for at, peer in enumerate(peers):
            x_copies[-1].append(
                remote(
                    xb.at[peer, :, cols],
                    x_in.at[me, :, cols],
                    x_send.at[portion, at],
                    x_recv.at[portion, at],
                    "req",
                    peer,
                )
            )
            x_copies[-1][-1].start()

    def state_copy(tile):
        lanes = pl.ds(pl.multiple_of(tile * 128, 128), 128)
        return pltpu.make_async_copy(state.at[:, lanes], held.at[tile], state_sem.at[tile])

    for w_at in range(chunks):
        for split in range(splits):
            at = split * chunks + w_at
            cols = pl.ds(at * span, span)
            pltpu.make_async_copy(dt_proj.at[:, cols], rate_w.at[:, cols], chunk_sem.at[at]).start()
            for tile in range(tiles):
                state_copy(at * tiles + tile).start()
    part[...] = jnp.zeros_like(part)
    for copy in loads:
        copy.wait()
    own_q.wait()
    for copy in q_copies:
        copy.wait_recv()

    cache_len = list_len * pool.shape[2]
    scale = 1.0 / math.sqrt(HEAD_SIZE)
    recent = kv_heads * steps
    all_rows = kv_heads * q_rows
    group_width = q_rows // steps
    token = lax.broadcasted_iota(jnp.int32, (all_rows, cache_len), 1)
    column = lax.broadcasted_iota(jnp.int32, (all_rows, recent), 1)
    row = lax.broadcasted_iota(jnp.int32, (all_rows, recent), 0)
    row_head = row // q_rows
    row_moment = (row - row_head * q_rows) // group_width
    seen = (column >= row_head * steps) & (column <= row_head * steps + row_moment)
    contract = (((1,), (1,)), ((), ()))
    together = 4

    def some_requests(at, carry):
        reqs = [at * together + offset for offset in range(together)]
        rows = reqs
        reqs = [order[slot] for slot in rows]
        scores, fresh = [], []
        for req, slot in zip(reqs, rows):
            keys = jnp.concatenate([pool[table[i, req], 0] for i in range(list_len)], axis=0)
            parts = [
                lax.dot_general(
                    q_in[slot, head * q_rows : (head + 1) * q_rows, :],
                    keys[:, head * HEAD_SIZE : (head + 1) * HEAD_SIZE],
                    contract,
                    preferred_element_type=jnp.float32,
                )
                for head in range(kv_heads)
            ]
            scores.append(jnp.concatenate(parts, axis=0))
            fresh.append(
                lax.dot_general(
                    q_in[slot, :all_rows, :],
                    q_in[slot, all_rows : all_rows + recent, :],
                    contract,
                    preferred_element_type=jnp.float32,
                )
            )
        weights = []
        for req, old, new in zip(reqs, scores, fresh):
            old = jnp.where(token < lengths[req], old * scale, -jnp.inf)
            new = jnp.where(seen, new * scale, -jnp.inf)
            top = jnp.maximum(
                jnp.max(old, axis=1, keepdims=True), jnp.max(new, axis=1, keepdims=True)
            )
            old = jnp.exp(old - top)
            new = jnp.exp(new - top)
            total = jnp.sum(old, axis=1, keepdims=True) + jnp.sum(new, axis=1, keepdims=True)
            weights.append((old.astype(jnp.bfloat16), new.astype(jnp.bfloat16), 1.0 / total))
        for req, slot, (old, new, inverse) in zip(reqs, rows, weights):
            values = jnp.concatenate([pool[table[i, req], 1] for i in range(list_len)], axis=0)
            parts = [
                jnp.dot(
                    old[head * q_rows : (head + 1) * q_rows, :],
                    values[:, head * HEAD_SIZE : (head + 1) * HEAD_SIZE],
                    preferred_element_type=jnp.float32,
                )
                for head in range(kv_heads)
            ]
            mixed = jnp.concatenate(parts, axis=0) + jnp.dot(
                new,
                q_in[slot, all_rows + recent : all_rows + 2 * recent, :],
                preferred_element_type=jnp.float32,
            )
            o_ready[slot] = (mixed * inverse).astype(jnp.bfloat16)
        return carry

    lax.fori_loop(0, local_reqs // together, some_requests, 0)

    own_x.wait()
    for portion in range(X_PARTS):
        for copy in x_copies[portion]:
            copy.wait_recv()
        for split in range(splits):

            def conv_chunk(at, carry):
                inner = pl.ds(pl.multiple_of(at * chunk, chunk), chunk)
                outer = pl.ds(pl.multiple_of(split * block_width + at * chunk, chunk), chunk)
                block = x_in[:, :, inner].reshape(n * BLOCK_ROWS, chunk)
                fresh = jnp.dot(place[split], block, preferred_element_type=jnp.float32)
                window = [conv_rows[row, :, outer].astype(jnp.float32) for row in range(taps - 1)]
                window += [fresh[t * local_reqs : (t + 1) * local_reqs] for t in range(steps)]
                for t in range(steps):
                    total = conv_bias[:, outer] + sum(
                        conv_weight[tap : tap + 1, outer] * window[t + tap] for tap in range(taps)
                    )
                    active = total / (1.0 + jnp.exp(-total))
                    conv_out[t * local_reqs : (t + 1) * local_reqs, outer] = active.astype(jnp.bfloat16)
                part[:, :proj_width] += lax.dot_general(
                    conv_out[:, outer],
                    proj_w[:, outer],
                    (((1,), (1,)), ((), ())),
                    preferred_element_type=jnp.float32,
                )
                return carry

            lax.fori_loop(
                portion * (half // chunk), (portion + 1) * (half // chunk), conv_chunk, 0
            )
        if portion == X_PARTS - 2:
            for copies in x_copies:
                for copy in copies:
                    copy.wait_send()
            for copy in o_copies:
                copy.start()
            own_o = pltpu.make_async_copy(
                o_ready.at[mine_rows], o_out.at[mine_rows], local_sem.at[2]
            )
            own_o.start()
    copies = []
    for step in range(1, width):
        peer = lax.rem(lane + step, width)
        copies.append(
            remote(
                part.at[pl.ds(pl.multiple_of(peer * piece, piece), piece)],
                gathered.at[step],
                rs_send.at[step],
                rs_recv.at[step],
                "tp",
                peer,
            )
        )
        copies[-1].start()
    mine = pl.ds(pl.multiple_of(lane * piece, piece), piece)
    gathered[0] = part[mine, :]
    for copy in copies:
        copy.wait()
    summed = gathered[0]
    for step in range(1, width):
        summed = summed + gathered[step]
    dt_low = summed[:, :rank_width]
    scale = lax.rsqrt(jnp.mean(dt_low * dt_low, axis=-1, keepdims=True) + EPSILON)
    normed[mine, :] = (dt_low * scale * dt_gain[...]).astype(jnp.bfloat16)
    coefs[mine, :] = summed[:, rank_width:]
    copies = []
    for step in range(1, width):
        peer = lax.rem(lane + step, width)
        for at, ref in enumerate((normed, coefs)):
            copies.append(
                remote(
                    ref.at[mine], ref.at[mine], ag_send.at[at, step], ag_recv.at[at, step], "tp", peer
                )
            )
            copies[-1].start()
    for copy in copies:
        copy.wait()
    for t in range(steps):
        at_rows = slice(t * local_reqs, (t + 1) * local_reqs)
        for entry in range(state_size):
            for wide, column in ((b_wide, entry), (c_wide, state_size + entry)):
                wide[t, entry] = jnp.broadcast_to(
                    coefs[at_rows, column : column + 1], (local_reqs, 128)
                )
    groups = local_reqs // 8

    def scan_chunk(w_at, carry):
        inner = pl.ds(pl.multiple_of(w_at * span, span), span)
        blocks = jnp.zeros((n * BLOCK_ROWS, span), jnp.float32)
        for split in range(splits):
            at = split * spans + w_at
            outer = pl.ds(pl.multiple_of(at * span, span), span)
            pltpu.make_async_copy(
                dt_proj.at[:, outer], rate_w.at[:, outer], chunk_sem.at[at]
            ).wait()
            raw = (
                jnp.dot(normed[...], rate_w[:, outer], preferred_element_type=jnp.float32)
                + dt_bias[:, outer]
            )
            rate = jnp.maximum(raw, 0.0) + jnp.log1p(jnp.exp(-jnp.abs(raw)))
            inputs = conv_out[:, outer].astype(jnp.float32)
            rates[...] = rate
            drives[...] = rate * inputs
            decay[...] = jnp.exp(a_log[:, outer]) * (-LOG2E)
            for tile in range(tiles):
                state_copy(at * tiles + tile).wait()

            def one_cell(cell, inner_carry):
                pair = cell // groups
                first = pl.multiple_of((cell - pair * groups) * 8, 8)
                subs = range(TILES_TOGETHER)
                lanes = [
                    pl.ds(pl.multiple_of((pair * TILES_TOGETHER + sub) * 128, 128), 128)
                    for sub in subs
                ]
                rows_at = [pl.ds(pl.multiple_of(t * local_reqs + first, 8), 8) for t in range(steps)]
                rate_t = [[rates[rows_at[t], lanes[sub]] for sub in subs] for t in range(steps)]
                drive_t = [[drives[rows_at[t], lanes[sub]] for sub in subs] for t in range(steps)]
                sums = [[jnp.zeros((8, 128), jnp.float32) for _ in subs] for _ in range(steps)]
                for entry in range(state_size):
                    entry_rows = pl.ds(first * state_size + entry, 8, stride=state_size)
                    hidden = [
                        held[at * tiles + pair * TILES_TOGETHER + sub, entry_rows, :] for sub in subs
                    ]
                    slope = [decay[entry : entry + 1, lanes[sub]] for sub in subs]
                    for t in range(steps):
                        b_now = b_wide[t, entry, pl.ds(first, 8), :]
                        c_now = c_wide[t, entry, pl.ds(first, 8), :]
                        for sub in subs:
                            hidden[sub] = (
                                jnp.exp2(rate_t[t][sub] * slope[sub]) * hidden[sub]
                                + drive_t[t][sub] * b_now
                            )
                            sums[t][sub] = sums[t][sub] + hidden[sub] * c_now
                for t in range(steps):
                    for sub in subs:
                        readings[rows_at[t], lanes[sub]] = sums[t][sub]
                return inner_carry

            lax.fori_loop(0, tiles // TILES_TOGETHER * groups, one_cell, 0)
            reading = (readings[...] + skip_d[:, outer] * inputs).astype(jnp.bfloat16)
            blocks = blocks + jnp.dot(
                place_back[split], reading, preferred_element_type=jnp.float32
            )
        ready[:, :, inner] = blocks.astype(jnp.bfloat16).reshape(n, BLOCK_ROWS, span)
        for step in range(1, n):
            peer = lax.rem(me + step, n)
            remote(
                ready.at[peer, :, inner],
                y_out.at[me, :, inner],
                y_send.at[step],
                y_recv.at[step],
                "req",
                peer,
            ).start()
        return carry

    lax.fori_loop(0, chunks, scan_chunk, 0)
    own_y = pltpu.make_async_copy(ready.at[me], y_out.at[me], local_sem.at[3])
    own_y.start()
    own_o.wait()
    for copy in o_copies:
        copy.wait()
    for step in range(1, n):
        peer = lax.rem(me + step, n)
        remote(
            ready.at[peer], y_out.at[me], y_send.at[step], y_recv.at[step], "req", peer
        ).wait()
    own_y.wait()


def scan_chunk_of(block_width):
    return min(256, block_width)


def decode(
    table,
    lengths,
    order,
    qb,
    xb,
    pool,
    conv_rows,
    place,
    place_back,
    conv_weight,
    conv_bias,
    x_proj,
    dt_gain,
    dt_proj,
    dt_bias,
    a_log,
    skip_d,
    state,
    kv_heads,
    q_rows,
    steps,
):
    n = xb.shape[0]
    width = lax.axis_size("tp")
    local_reqs = table.shape[1]
    rows = place.shape[1]
    state_size, channels = a_log.shape
    rank_width = dt_gain.shape[1]
    wide = rank_width + 128
    span = scan_chunk_of(xb.shape[2])
    dma = pltpu.SemaphoreType.DMA
    smem = pl.BlockSpec(memory_space=pltpu.SMEM)
    outs = jax.ShapeDtypeStruct((local_reqs, kv_heads * q_rows, HEAD_SIZE), jnp.bfloat16)
    return pl.pallas_call(
        functools.partial(decode_kernel, kv_heads, q_rows, steps),
        out_shape=(outs, jax.ShapeDtypeStruct(xb.shape, jnp.bfloat16)),
        in_specs=[smem] * 3 + [ANY] * 15,
        out_specs=(ANY, ANY),
        scratch_shapes=[
            like(pool),
            like(conv_rows),
            like(place),
            like(place_back),
            like(conv_weight),
            like(conv_bias),
            like(dt_gain),
            like(dt_bias),
            like(a_log),
            like(skip_d),
            like(x_proj),
            dma((11,)),
            like(qb),
            like(xb),
            like(outs),
            pltpu.VMEM((rows, channels), jnp.bfloat16),
            pltpu.VMEM((rows, wide), jnp.float32),
            pltpu.VMEM((width, rows // width, wide), jnp.float32),
            pltpu.VMEM((rows, rank_width), jnp.bfloat16),
            pltpu.VMEM((rows, 128), jnp.float32),
            pltpu.VMEM((steps, state_size, local_reqs, 128), jnp.float32),
            pltpu.VMEM((steps, state_size, local_reqs, 128), jnp.float32),
            pltpu.VMEM((state_size, span), jnp.float32),
            pltpu.VMEM((channels // 128, local_reqs * state_size, 128), jnp.float32),
            like(dt_proj),
            pltpu.VMEM((rows, span), jnp.float32),
            pltpu.VMEM((rows, span), jnp.float32),
            pltpu.VMEM((rows, span), jnp.float32),
            like(xb),
            dma((n,)),
            dma((n,)),
            dma((X_PARTS, n)),
            dma((X_PARTS, n)),
            dma((n,)),
            dma((n,)),
            dma((n,)),
            dma((n,)),
            dma((4,)),
            dma((channels // span,)),
            dma((channels // 128,)),
            dma((width,)),
            dma((width,)),
            dma((2, width)),
            dma((2, width)),
        ],
        compiler_params=pltpu.CompilerParams(
            collective_id=0, has_side_effects=True, vmem_limit_bytes=VMEM_LIMIT
        ),
    )(
        table,
        lengths,
        order,
        qb,
        xb,
        pool,
        conv_rows,
        place,
        place_back,
        conv_weight,
        conv_bias,
        x_proj,
        dt_gain,
        dt_proj,
        dt_bias,
        a_log,
        skip_d,
        state,
    )


def per_device(
    queries,
    new_kv,
    prefill_page_pool,
    page_table,
    prompt_len,
    dest_device,
    ssm_state,
    conv_state,
    mamba_x,
    mamba_z,
    conv_weight,
    conv_bias,
    x_proj,
    dt_gain,
    dt_proj,
    dt_bias,
    a_log,
    skip_d,
):
    n = lax.axis_size("req")
    local_reqs = dest_device.shape[0]
    steps = queries.shape[0]
    channels = mamba_x.shape[2]
    kv_heads = prefill_page_pool.shape[3] // HEAD_SIZE
    group_width = queries.shape[2] // HEAD_SIZE // kv_heads
    q_rows = steps * group_width
    state_size = a_log.shape[0]
    share = local_reqs // n
    splits = BLOCK_ROWS // (steps * share)
    block_width = channels // splits
    index = jnp.arange(local_reqs, dtype=jnp.int32)
    same = dest_device[:, None] == dest_device[None, :]
    rank = jnp.sum((same & (index[None, :] < index[:, None])).astype(jnp.int32), axis=1)
    slots = dest_device * share + rank
    order = jnp.sum(jnp.where(slots[:, None] == index[None, :], index[:, None], 0), axis=0)
    times = jnp.arange(steps, dtype=jnp.int32)
    split_ids = jnp.arange(splits, dtype=jnp.int32)
    block_row = dest_device * BLOCK_ROWS + rank * splits
    block_row = (
        block_row[None, None, :]
        + times[None, :, None] * (share * splits)
        + split_ids[:, None, None]
    ).reshape(splits, steps * local_reqs)
    block_ids = jnp.arange(n * BLOCK_ROWS, dtype=jnp.int32)
    place = (block_row[:, :, None] == block_ids[None, None, :]).astype(jnp.bfloat16)
    place_back = (block_row[:, None, :] == block_ids[None, :, None]).astype(jnp.bfloat16)

    decode_row = (
        index[None, :] // share * BLOCK_ROWS
        + (times[:, None] * share + index[None, :] % share) * splits
    ).reshape(1, steps * local_reqs) + split_ids[:, None]
    home = (decode_row[:, :, None] == block_ids[None, None, :]).astype(jnp.bfloat16)
    flat_x = mamba_x.reshape(steps * local_reqs, channels)
    xb = sum(
        jnp.einsum("pb,pc->bc", home[at], flat_x[:, at * block_width : (at + 1) * block_width])
        for at in range(splits)
    ).reshape(n, BLOCK_ROWS, block_width)
    q_part = jnp.transpose(
        queries.reshape(steps, local_reqs, kv_heads, group_width, HEAD_SIZE), (1, 2, 0, 3, 4)
    ).reshape(local_reqs, kv_heads * q_rows, HEAD_SIZE)
    kv_part = jnp.transpose(
        new_kv.reshape(steps, local_reqs, 2, kv_heads, HEAD_SIZE), (1, 2, 3, 0, 4)
    ).reshape(local_reqs, 2 * kv_heads * steps, HEAD_SIZE)
    slabs = jnp.concatenate([q_part, kv_part], axis=1)
    o_back, y_back = decode(
        page_table.T,
        prompt_len,
        order,
        slabs,
        xb,
        prefill_page_pool,
        jnp.transpose(conv_state, (1, 0, 2)),
        place,
        place_back,
        conv_weight,
        conv_bias[None],
        x_proj.T,
        dt_gain[None],
        dt_proj,
        dt_bias[None],
        a_log,
        skip_d[None],
        ssm_state.reshape(local_reqs * state_size, channels),
        kv_heads,
        q_rows,
        steps,
    )
    attn_out = jnp.transpose(
        o_back.reshape(local_reqs, kv_heads, steps, group_width, HEAD_SIZE), (2, 0, 1, 3, 4)
    ).reshape(queries.shape)
    flat_y = y_back.reshape(n * BLOCK_ROWS, block_width)
    reading = jnp.concatenate(
        [
            jnp.einsum("pb,bc->pc", home[at], flat_y, preferred_element_type=jnp.float32)
            for at in range(splits)
        ],
        axis=1,
    )
    gate_values = jax.nn.silu(mamba_z.astype(jnp.float32)).reshape(reading.shape)
    mamba_out = (reading * gate_values).astype(jnp.bfloat16).reshape(mamba_x.shape)
    return (attn_out, mamba_out)


def solution(mesh):
    return jax.shard_map(
        per_device,
        mesh=mesh,
        in_specs=(
            P(None, "req", "tp"),
            P(None, "req", None, "tp"),
            P("req", None, None, "tp"),
            P("req", None),
            P("req"),
            P("req"),
            P("req", None, "tp"),
            P("req", None, "tp"),
            P(None, "req", "tp"),
            P(None, "req", "tp"),
            P(None, "tp"),
            P("tp"),
            P("tp", None),
            P(),
            P(None, "tp"),
            P("tp"),
            P(None, "tp"),
            P("tp"),
        ),
        out_specs=(P(None, "req", "tp"), P(None, "req", "tp")),
        check_vma=False,
    )
```
